32 devices in a mesh: seq: 8 (over y, x, core), head: 4 (over z).
Axes of the slice: x: 2, y: 2, z: 4, core: 2. Of those that a mesh axis runs over, the one named last changes fastest.
Arguments:
- features: bfloat16 [4096, 4096], P('seq', 'head'), may hold values from -6 to 6
- key_weight: bfloat16 [4096, 4096], P(None, 'head'), may hold values from -0.09375 to 0.09375
- value_weight: bfloat16 [4096, 4096], P(None, 'head'), may hold values from -0.09375 to 0.09375
- queries: bfloat16 [4096, 4096], P('seq', 'head'), may hold values from -6 to 6
- log_decay: float32 [4096, 32], P('seq', 'head'), may hold values from -1.5 to 0, as said below
- out_grad: bfloat16 [4096, 4096], P('seq', 'head'), may hold values from -6 to 6
Outputs:
- attended: bfloat16 [4096, 4096], P('seq', 'head')
- query_grad: bfloat16 [4096, 4096], P('seq', 'head')
- feature_grad: bfloat16 [4096, 4096], P('seq', 'head')
- key_weight_grad: float32 [4096, 4096], P('seq', 'head')
- value_weight_grad: float32 [4096, 4096], P('seq', 'head')
The draws below stay inside these ranges and needn't reach their ends.
Inputs may be any that keep to these rules, and one draw needn't show every extreme that they name: `log_decay`: every entry is negative.
All inputs are finite; a program needn't handle non-finite values.
Results may differ from the reference program's by a relative error of at most 0.014.
Values may be sent and summed in bfloat16 or wider, within the bound.
No kernel may reach another device: no remote copies, remote signals or barrier semaphores. Data moves between devices by JAX's collectives and lax.ppermute only.
A program may use at most 192 MiB of HBM per device.

```python
import math
import jax
import jax.numpy as jnp
from jax import lax

D = 4096
HEAD_COUNT = 32
HEAD_DIM = 128
TOK_DEV = 512
PROJ = 4096
TOKEN_COUNT = 4096


def draw_log_decay(key, part):
    key_matrix = jax.random.split(key, 7)
    fast_share = 0.5
    fast = jax.random.uniform(key_matrix[0], (HEAD_COUNT,), jnp.float32) < fast_share
    fast_rate = jnp.exp(jax.random.uniform(key_matrix[1], (HEAD_COUNT,), jnp.float32, math.log(1.0 / 50.0), math.log(1.0 / 30.0)))
    slow_rate = jnp.exp(jax.random.uniform(key_matrix[2], (HEAD_COUNT,), jnp.float32, math.log(0.1), math.log(0.5))) / TOKEN_COUNT
    rate = jnp.where(fast, fast_rate, slow_rate)
    blocks = TOKEN_COUNT // TOK_DEV
    block_factor = jnp.exp(jax.random.uniform(key_matrix[3], (blocks, HEAD_COUNT), jnp.float32, math.log(0.5), math.log(2.0)))
    per_token = jnp.repeat(block_factor, TOK_DEV, axis=0)
    rough = jax.random.uniform(key_matrix[4], (TOKEN_COUNT, HEAD_COUNT), jnp.float32, 0.5, 1.5)
    spike_position = jax.random.randint(key_matrix[5], (2, HEAD_COUNT), 0, TOKEN_COUNT)
    layer_depth = jax.random.uniform(key_matrix[6], (2, HEAD_COUNT), jnp.float32, 0.22, 0.69)
    match_count = (jnp.arange(TOKEN_COUNT)[:, None, None] == spike_position[None]).astype(jnp.float32) * layer_depth[None]
    return -(rate[None, :] * per_token * rough + jnp.sum(match_count, axis=1))


def block_scale(key, shape, pieces, least, top_value):
    level, own = 1.0, jax.random.fold_in(key, 6)
    for position, shards_of in pieces:
        heights = jnp.exp(jax.random.uniform(jax.random.fold_in(own, position), (shards_of,), jnp.float32, least / len(pieces), top_value / len(pieces)))
        level = level * jnp.repeat(heights, shape[position] // shards_of).reshape([-1 if axis == position else 1 for axis in range(len(shape))])
    return level


def noise(rng, extent, scale, most, shards=(), held_as=jnp.bfloat16):
    entries = jax.random.normal(rng, extent, jnp.float32) * scale
    if len(shards) > 0:
        entries = block_scale(rng, extent, shards, -0.22, 0.18) * entries
    return jnp.clip(entries, min=-most, max=most).astype(held_as)


def setup_inputs(seed: int = 0) -> dict:
    key_list = jax.random.split(jax.random.key(seed), 7)
    features = noise(key_list[0], (TOKEN_COUNT, D), 1.0, 6.0, ((0, 8), (1, 4)))
    key_weight = noise(key_list[1], (D, PROJ), D ** -0.5, 0.09375, ((1, 4),))
    value_weight = noise(key_list[2], (D, PROJ), D ** -0.5, 0.09375, ((1, 4),))
    queries = noise(key_list[3], (TOKEN_COUNT, PROJ), 1.0, 6.0, ((0, 8), (1, 4)))
    log_decay = draw_log_decay(jax.random.fold_in(key_list[6], 71), 0)
    out_grad = noise(key_list[5], (TOKEN_COUNT, PROJ), 1.0, 6.0, ((0, 8), (1, 4)))
    return dict(features=features, key_weight=key_weight, value_weight=value_weight, queries=queries, log_decay=log_decay, out_grad=out_grad)


def block_decay(decay_block):
    cum = jnp.cumsum(decay_block, axis=0)
    positions = jnp.arange(decay_block.shape[0])
    causal = (positions[:, None] >= positions[None, :])[None]
    gap = jnp.transpose(cum[:, None, :] - cum[None, :, :], (2, 0, 1))
    decay = jnp.where(causal, jnp.exp(jnp.where(causal, gap, 0.0)), 0.0)
    return (cum, decay)

def forward_block(state, item):
    query_block, key_block, value_block, decay_block = item
    cum, decay = block_decay(decay_block)
    query_float = query_block.astype(jnp.float32)
    key_float = key_block.astype(jnp.float32)
    value_float = value_block.astype(jnp.float32)
    scores = jnp.einsum('the,she->hts', query_float, key_float)
    weights = (scores * decay).astype(jnp.bfloat16)
    local_mix = jnp.einsum('hts,she->the', weights.astype(jnp.float32), value_float)
    carried = jnp.exp(cum)[:, :, None] * jnp.einsum('the,hef->thf', query_float, state, precision=lax.Precision.HIGHEST)
    tail = jnp.exp(cum[-1][None, :] - cum)
    local_state = jnp.einsum('she,shf->hef', key_float * tail[:, :, None], value_float, precision=lax.Precision.HIGHEST)
    new_state = jnp.exp(cum[-1])[:, None, None] * state + local_state
    return (new_state, (state, local_mix + carried))

def backward_block(outgoing, item):
    query_block, key_block, value_block, decay_block, grad_block, state = item
    cum, decay = block_decay(decay_block)
    query_float = query_block.astype(jnp.float32)
    key_float = key_block.astype(jnp.float32)
    value_float = value_block.astype(jnp.float32)
    scores = jnp.einsum('the,she->hts', query_float, key_float)
    weights = (scores * decay).astype(jnp.bfloat16).astype(jnp.float32)
    grad_round = grad_block.astype(jnp.bfloat16).astype(jnp.float32)
    pair_scores = jnp.einsum('the,she->hts', grad_round, value_float)
    grad_weights = (pair_scores * decay).astype(jnp.bfloat16).astype(jnp.float32)
    growth = jnp.exp(cum)
    tail = jnp.exp(cum[-1][None, :] - cum)
    highest = lax.Precision.HIGHEST
    query_grad = jnp.einsum('hts,she->the', grad_weights, key_float) + growth[:, :, None] * jnp.einsum('thf,hef->the', grad_block, state, precision=highest)
    key_grad = jnp.einsum('hts,the->she', grad_weights, query_float) + tail[:, :, None] * jnp.einsum('shf,hef->she', value_float, outgoing, precision=highest)
    value_grad = jnp.einsum('hts,thf->shf', weights, grad_round) + tail[:, :, None] * jnp.einsum('she,hef->shf', key_float, outgoing, precision=highest)
    reverse_local = jnp.einsum('the,thf->hef', query_float * growth[:, :, None], grad_block, precision=highest)
    new_outgoing = jnp.exp(cum[-1])[:, None, None] * outgoing + reverse_local
    return (new_outgoing, (query_grad.astype(jnp.bfloat16), key_grad.astype(jnp.bfloat16), value_grad.astype(jnp.bfloat16)))

def reference(features, key_weight, value_weight, queries, log_decay, out_grad):
    key_matrix = jnp.dot(features, key_weight, preferred_element_type=jnp.float32).astype(jnp.bfloat16)
    values = jnp.dot(features, value_weight, preferred_element_type=jnp.float32).astype(jnp.bfloat16)
    blocks = TOKEN_COUNT // TOK_DEV
    shape = (blocks, TOK_DEV, HEAD_COUNT, HEAD_DIM)
    query_blocks = queries.reshape(shape)
    key_blocks = key_matrix.reshape(shape)
    value_blocks = values.reshape(shape)
    decay_blocks = log_decay.reshape(blocks, TOK_DEV, HEAD_COUNT)
    start_state = jnp.zeros((HEAD_COUNT, HEAD_DIM, HEAD_DIM), jnp.float32)
    last_state, (states, mixed) = lax.scan(forward_block, start_state, (query_blocks, key_blocks, value_blocks, decay_blocks))
    scale = lax.rsqrt(lax.optimization_barrier(jnp.mean(mixed * mixed, axis=-1, keepdims=True)) + 1e-06)
    attended = (mixed * scale).astype(jnp.bfloat16).reshape(TOKEN_COUNT, PROJ)
    grad_float = out_grad.reshape(shape).astype(jnp.float32)
    projection = lax.optimization_barrier(jnp.mean(grad_float * mixed, axis=-1, keepdims=True))
    head_gradient = scale * grad_float - mixed * scale * scale * scale * projection
    first_out, (query_grad, key_grad, value_grad) = lax.scan(backward_block, start_state, (query_blocks, key_blocks, value_blocks, decay_blocks, head_gradient, states), reverse=True)
    key_grad = key_grad.reshape(TOKEN_COUNT, PROJ)
    value_grad = value_grad.reshape(TOKEN_COUNT, PROJ)
    feature_grad = jnp.dot(key_grad, key_weight.T, preferred_element_type=jnp.float32) + jnp.dot(value_grad, value_weight.T, preferred_element_type=jnp.float32)
    both_grads = jnp.concatenate([key_grad, value_grad], axis=1).reshape(blocks, TOK_DEV, 2 * PROJ)
    feature_blocks = features.reshape(blocks, TOK_DEV, D)

    def add_block(total, item):
        feature_block, grad_block = item
        term = jnp.dot(feature_block.T, grad_block, preferred_element_type=jnp.float32).astype(jnp.bfloat16)
        term = lax.optimization_barrier(term)
        return (total + term.astype(jnp.float32), None)
    summed, unused = lax.scan(add_block, jnp.zeros((D, 2 * PROJ), jnp.float32), (feature_blocks, both_grads))
    summed = summed * TOKEN_COUNT ** (-0.5)
    return (attended, query_grad.reshape(TOKEN_COUNT, PROJ), feature_grad.astype(jnp.bfloat16), summed[:, :PROJ], summed[:, PROJ:])
```

```python
import functools

import jax
import jax.numpy as jnp
from jax import lax
from jax.experimental import pallas as pl
from jax.experimental.pallas import tpu as pltpu
from jax.sharding import PartitionSpec as P

BF = jnp.bfloat16
F32 = jnp.float32
NT = (((1,), (1,)), ((), ()))
TN = (((0,), (0,)), ((), ()))
VMEM_LIMIT = 48 * 1024 * 1024
SPLIT = 2


def dot(a, b):
    return jnp.dot(a, b, preferred_element_type=F32)


def dot_nt(a, b):
    return lax.dot_general(a, b, NT, preferred_element_type=F32)


def dot_tn(a, b):
    return lax.dot_general(a, b, TN, preferred_element_type=F32)


def params(**more):
    return pltpu.CompilerParams(vmem_limit_bytes=VMEM_LIMIT, **more)


def cost(flops, data):
    return pl.CostEstimate(flops=flops, bytes_accessed=data, transcendentals=0)


def last_kv_kernel(width, pieces, index_ref, *refs):
    parts = refs[:pieces]
    kw_ref, vw_ref, ka_ref, va_ref, tail_ref, k_ref, v_ref, s_ref, held = refs[pieces:]

    @pl.when(pl.program_id(0) == 0)
    def _():
        rows = held.shape[0] // (pieces // 2)
        for i in range(pieces // 2):
            held[i * rows : (i + 1) * rows, :] = parts[2 * i][...] + parts[2 * i + 1][...]

    f = held[...]
    keys = (ka_ref[...] + dot(f, kw_ref[...])).astype(BF)
    values = (va_ref[...] + dot(f, vw_ref[...])).astype(BF)
    k_ref[...] = keys
    v_ref[...] = values
    scaled = (keys.astype(F32) * tail_ref[...]).astype(BF)
    for i in range(s_ref.shape[0]):
        cut = slice(i * width, (i + 1) * width)
        s_ref[i] = dot_tn(scaled[:, cut], values[:, cut]).astype(BF)


def last_kv(parts, index, key_weight, value_weight, key_sum, value_sum, tail, width, per):
    tokens, proj = key_sum.shape
    depth = parts[0].shape[1]
    cols = width * per
    whole = [pl.BlockSpec(p.shape, lambda j, d: (0, 0)) for p in parts]
    weight = pl.BlockSpec((depth, cols), lambda j, d: (d[0], j))
    column = pl.BlockSpec((tokens, cols), lambda j, d: (0, j))
    state = pl.BlockSpec((per, width, width), lambda j, d: (j, 0, 0))
    return pl.pallas_call(
        functools.partial(last_kv_kernel, width, len(parts)),
        grid_spec=pltpu.PrefetchScalarGridSpec(
            num_scalar_prefetch=1,
            grid=(proj // cols,),
            in_specs=whole + [weight, weight, column, column, column],
            out_specs=[column, column, state],
            scratch_shapes=[pltpu.VMEM((tokens, depth), BF)],
        ),
        out_shape=[
            jax.ShapeDtypeStruct((tokens, proj), BF),
            jax.ShapeDtypeStruct((tokens, proj), BF),
            jax.ShapeDtypeStruct((proj // width, width, width), BF),
        ],
        compiler_params=params(),
        cost_estimate=cost(4 * tokens * depth * proj, 12 * tokens * proj + 4 * depth * proj),
        name="last_kv",
    )(index, *parts, key_weight, value_weight, key_sum, value_sum, tail)


def causal_tiles(tokens):
    tile = min(256, tokens)
    for row in range(tokens // tile):
        yield slice(row * tile, (row + 1) * tile), slice(0, (row + 1) * tile)


def anti_tiles(tokens):
    tile = min(256, tokens)
    for row in range(tokens // tile):
        yield slice(row * tile, (row + 1) * tile), slice(row * tile, tokens)


def local_kernel(width, q_ref, k_ref, v_ref, dec_ref, mix_ref):
    for i in range(dec_ref.shape[0]):
        cut = slice(i * width, (i + 1) * width)
        for rows, seen in causal_tiles(q_ref.shape[0]):
            scores = dot_nt(q_ref[rows, cut], k_ref[seen, cut])
            weights = (scores * dec_ref[i, rows, seen].astype(F32)).astype(BF)
            mix_ref[rows, cut] = dot(weights, v_ref[seen, cut])


def norm_kernel(width, q_ref, g_ref, mix_ref, grow_ref, qt_ref, s_ref, att_ref, hg_ref, r_ref):
    for i in range(s_ref.shape[0]):
        cut = slice(i * width, (i + 1) * width)
        mixed = mix_ref[:, cut] + grow_ref[:, cut] * dot(q_ref[:, cut], s_ref[i])
        grad = g_ref[:, cut].astype(F32)
        scale = lax.rsqrt(jnp.mean(mixed * mixed, axis=-1, keepdims=True) + 1e-06)
        projection = jnp.mean(grad * mixed, axis=-1, keepdims=True)
        att_ref[:, cut] = (mixed * scale).astype(BF)
        head_grad = (scale * grad - mixed * (scale * scale * scale * projection)).astype(BF)
        hg_ref[:, cut] = head_grad
        r_ref[i] = dot(qt_ref[cut, :], head_grad).astype(BF)


def back_kernel(
    width, q_ref, k_ref, v_ref, hg_ref, dec_ref, dect_ref, grow_ref, s_ref, qg_ref, kg_ref, vg_ref
):
    tokens = q_ref.shape[0]
    for i in range(s_ref.shape[0]):
        cut = slice(i * width, (i + 1) * width)
        for rows, seen in causal_tiles(tokens):
            pairs = dot_nt(hg_ref[rows, cut], v_ref[seen, cut])
            pairs = (pairs * dec_ref[i, rows, seen].astype(F32)).astype(BF)
            carried = grow_ref[rows, cut] * dot_nt(hg_ref[rows, cut], s_ref[i])
            qg_ref[rows, cut] = (dot(pairs, k_ref[seen, cut]) + carried).astype(BF)
        for rows, seen in anti_tiles(tokens):
            decay = dect_ref[i, rows, seen].astype(F32)
            pairs = (dot_nt(v_ref[rows, cut], hg_ref[seen, cut]) * decay).astype(BF)
            kg_ref[rows, cut] = dot(pairs, q_ref[seen, cut])
            weights = (dot_nt(k_ref[rows, cut], q_ref[seen, cut]) * decay).astype(BF)
            vg_ref[rows, cut] = dot(weights, hg_ref[seen, cut])


def close_kernel(width, k_ref, v_ref, kl_ref, vl_ref, tail_ref, r_ref, kg_ref, vg_ref):
    for i in range(r_ref.shape[0]):
        cut = slice(i * width, (i + 1) * width)
        tail = tail_ref[:, cut]
        kg_ref[:, cut] = (kl_ref[:, cut] + tail * dot_nt(v_ref[:, cut], r_ref[i])).astype(BF)
        vg_ref[:, cut] = (vl_ref[:, cut] + tail * dot(k_ref[:, cut], r_ref[i])).astype(BF)


def per_head(kernel, args, kinds, outs, heads, width, per, flops, name):
    tokens = args[0].shape[0]
    specs = {
        "col": pl.BlockSpec((tokens, width * per), lambda j: (0, j)),
        "row": pl.BlockSpec((width * per, tokens), lambda j: (j, 0)),
        "dec": pl.BlockSpec((per, tokens, tokens), lambda j: (j, 0, 0)),
        "state": pl.BlockSpec((per, width, width), lambda j: (j, 0, 0)),
    }
    shapes = {"col": (tokens, heads * width), "state": (heads, width, width)}
    data = sum(a.size * a.dtype.itemsize for a in args)
    return pl.pallas_call(
        functools.partial(kernel, width),
        grid=(heads // per,),
        in_specs=[specs[k] for k in kinds],
        out_specs=[specs[k] for k, _ in outs],
        out_shape=[jax.ShapeDtypeStruct(shapes[k], t) for k, t in outs],
        compiler_params=params(),
        cost_estimate=cost(flops, data),
        name=name,
    )(*args)


def feature_kernel(count, index_ref, kg_ref, vg_ref, kw_ref, vw_ref, *refs):
    total = dot_nt(kg_ref[...], kw_ref[...]) + dot_nt(vg_ref[...], vw_ref[...])
    for r in refs[:count]:
        total += r[...].astype(F32)
    refs[count][...] = total.astype(BF)


def feature_term(index, key_grad, value_grad, key_weight, value_weight, adds, span):
    tokens, proj = key_grad.shape
    tile = min(256, span)
    steps = span // tile
    whole = pl.BlockSpec((tokens, proj), lambda j, d: (0, 0))
    weight = pl.BlockSpec((tile, proj), lambda j, d: (d[0] * steps + j, 0))
    column = pl.BlockSpec((tokens, tile), lambda j, d: (0, j))
    return pl.pallas_call(
        functools.partial(feature_kernel, len(adds)),
        grid_spec=pltpu.PrefetchScalarGridSpec(
            num_scalar_prefetch=1,
            grid=(steps,),
            in_specs=[whole, whole, weight, weight] + [column] * len(adds),
            out_specs=column,
        ),
        out_shape=jax.ShapeDtypeStruct((tokens, span), BF),
        compiler_params=params(),
        cost_estimate=cost(4 * tokens * proj * span, 4 * proj * (tokens + span)),
        name="feature_term",
    )(index, key_grad, value_grad, key_weight, value_weight, *adds)


def weight_kernel(count, index_ref, fo_ref, fp_ref, go_ref, gp_ref, *refs):
    total = dot(fo_ref[...], go_ref[...]) + dot(fp_ref[...], gp_ref[...])
    for r in refs[:count]:
        total += r[...].astype(F32)
    refs[count][...] = total.astype(refs[count].dtype)


def weight_term(index, own_t, partner_t, own_grad, partner_grad, adds, span, kind):
    tokens, proj = own_grad.shape
    tile = min(256, proj)
    rows = pl.BlockSpec((span, tokens), lambda j, d: (d[0], 0))
    grad = pl.BlockSpec((tokens, tile), lambda j, d: (0, j))
    column = pl.BlockSpec((span, tile), lambda j, d: (0, j))
    return pl.pallas_call(
        functools.partial(weight_kernel, len(adds)),
        grid_spec=pltpu.PrefetchScalarGridSpec(
            num_scalar_prefetch=1,
            grid=(proj // tile,),
            in_specs=[rows, rows, grad, grad] + [column] * len(adds),
            out_specs=column,
        ),
        out_shape=jax.ShapeDtypeStruct((span, proj), kind),
        compiler_params=params(),
        cost_estimate=cost(4 * tokens * proj * span, 4 * tokens * (proj + span)),
        name="weight_term",
    )(index, own_t, partner_t, own_grad, partner_grad, *adds)


def merge_states(earlier, later):
    return (earlier[0] * later[0], later[0][:, None, None] * earlier[1] + later[1])


def entering(x, axis, backward):
    count = lax.axis_size(axis)
    place = lax.axis_index(axis)
    ahead = count - 1 - place if backward else place
    gathered = tuple(lax.all_gather(a.astype(BF), axis) for a in x)
    state = (jnp.ones_like(x[0]), jnp.zeros_like(x[1]))

    def one(hop, state):
        source = count - 1 - hop if backward else hop
        item = tuple(
            lax.dynamic_index_in_dim(a, source, 0, False).astype(own.dtype)
            for a, own in zip(gathered, x)
        )
        return merge_states(state, item)

    return lax.fori_loop(0, ahead, one, state)[1].astype(BF)


def swap(x, bit, keep=None):
    pairs = [(s, s ^ bit) for s in range(8) if keep is None or keep(s)]
    return lax.ppermute(x, "seq", pairs)


def gather_totals(own):
    place = lax.axis_index("seq")
    held = own[None]
    for bit in (1, 2, 4):
        other = swap(held, bit)
        upper = (place & bit) != 0
        held = jnp.concatenate(
            [jnp.where(upper, other, held), jnp.where(upper, held, other)], axis=0
        )
    return held


def entering_chips(state, totals, backward):
    place = lax.axis_index("seq")
    chip, core = place // 2, lax.rem(place, 2)
    half = state.shape[0] // 2
    partner = swap(state, 1)
    low = jnp.where(core == 0, state, partner)
    high = jnp.where(core == 0, partner, state)
    first, last = (high, low) if backward else (low, high)
    chip_totals = totals.reshape(4, 2, -1)
    mine = chip_totals[chip]
    factor = jnp.exp(mine[0 if backward else 1])
    total = (factor[:, None, None] * first.astype(F32) + last.astype(F32)).astype(BF)
    sent = lax.dynamic_slice_in_dim(total, core * half, half, 0)
    sums = jnp.sum(chip_totals, axis=1)
    numbers = jnp.arange(4)
    entered = jnp.zeros(sent.shape, F32)
    for bit in (2, 4, 6):
        top = 4 if bit & 4 else 2
        keep = (lambda s: (s & top) != 0) if backward else (lambda s: (s & top) == 0)
        got = swap(sent, bit, keep)
        source = chip ^ (bit // 2)
        between = (numbers > jnp.minimum(source, chip)) & (numbers < jnp.maximum(source, chip))
        gap = jnp.exp(jnp.sum(jnp.where(between[:, None], sums, 0.0), axis=0))
        gap = lax.dynamic_slice_in_dim(gap, core * half, half, 0)
        entered = entered + gap[:, None, None] * got.astype(F32)
    mine_half = entered.astype(BF)
    other_half = swap(mine_half, 1)
    whole = jnp.concatenate(
        [
            jnp.where(core == 0, mine_half, other_half),
            jnp.where(core == 0, other_half, mine_half),
        ],
        axis=0,
    )
    step = jnp.exp(mine[1 if backward else 0])[:, None, None] * whole.astype(F32) + first.astype(F32)
    return jnp.where(core == (0 if backward else 1), step.astype(BF), whole)


def line_pairs(count, step, up):
    if up:
        return [(i, i + 1) for i in range(step - 1, count - 1)]
    return [(i, i - 1) for i in range(1, count - step + 1)]


def scatter_pairs(count, step, up):
    if up:
        return [(i, i + 1) for i in range(0, min(step, count - 1))]
    return [(i, i - 1) for i in range(max(1, count - step), count)]


def per_device(features, key_weight, value_weight, queries, log_decay, out_grad):
    tokens, proj = queries.shape
    depth = features.shape[1]
    model = key_weight.shape[0]
    heads = log_decay.shape[1]
    width = proj // heads
    per = 2 if heads % 2 == 0 else 1
    count = lax.axis_size("head")
    blocks = lax.axis_size("seq")
    here = lax.axis_index("head")
    place = lax.axis_index("seq")
    chips = blocks == 8 and model == 8 * 512 and count == 4

    cum = jnp.cumsum(log_decay, axis=0)
    total = cum[-1]
    growth = jnp.exp(cum)
    tail = jnp.exp(total[None, :] - cum)
    grow = jnp.repeat(growth, width, axis=1)
    tails = jnp.repeat(tail, width, axis=1)
    positions = jnp.arange(tokens)
    causal = (positions[:, None] >= positions[None, :])[None]
    cum_t = cum.T
    gap = cum_t[:, :, None] - cum_t[:, None, :]
    decay = jnp.where(causal, jnp.exp(jnp.where(causal, gap, 0.0)), 0.0).astype(BF)
    causal_t = (positions[:, None] <= positions[None, :])[None]
    decay_t = jnp.where(causal_t, jnp.exp(jnp.where(causal_t, -gap, 0.0)), 0.0).astype(BF)
    query_t = (queries.astype(F32) * grow).astype(BF).T

    rows = tokens // SPLIT
    parts = [features[i * rows : (i + 1) * rows] for i in range(SPLIT)]
    up = list(parts)
    down = list(parts)
    gathered = jnp.zeros((tokens, model), BF)

    def place_shard(gathered, shard, index):
        return lax.dynamic_update_slice_in_dim(gathered, shard, index * depth, 1)

    def rows_of(weight, index):
        return lax.dynamic_slice_in_dim(weight, index * depth, depth, 0)

    key_sum = dot(features, rows_of(key_weight, here))
    value_sum = dot(features, rows_of(value_weight, here))
    gathered = place_shard(gathered, features, here)
    for step in range(1, count):
        up = [lax.ppermute(u, "head", line_pairs(count, step, True)) for u in up]
        down = [lax.ppermute(d, "head", line_pairs(count, step, False)) for d in down]
        if 2 * step >= count:
            index = jnp.where(here >= step, here - step, jnp.minimum(here + step, count - 1))
            valid = (here >= step) | (here + step <= count - 1)
            shards = [(jnp.concatenate([u + d for u, d in zip(up, down)], axis=0), index, valid)]
        else:
            shards = [
                (jnp.concatenate(up, axis=0), jnp.maximum(here - step, 0), here >= step),
                (
                    jnp.concatenate(down, axis=0),
                    jnp.minimum(here + step, count - 1),
                    here + step <= count - 1,
                ),
            ]
        for shard, index, valid in shards:
            if step < count - 1:
                key_sum = key_sum + dot(shard, rows_of(key_weight, index))
                value_sum = value_sum + dot(shard, rows_of(value_weight, index))
            old = lax.dynamic_slice_in_dim(gathered, index * depth, depth, 1)
            gathered = place_shard(gathered, jnp.where(valid, shard, old), index)
    pieces = [x for pair in zip(up, down) for x in pair]
    keys, values, local_state = last_kv(
        pieces, index[None], key_weight, value_weight, key_sum, value_sum, tails, width, per
    )

    if chips:
        totals = gather_totals(total)
        incoming = entering_chips(local_state, totals, False)
    else:
        incoming = entering((jnp.exp(total), local_state.astype(F32)), "seq", False)

    pair_flops = 2 * heads * tokens * tokens * width
    each = functools.partial(per_head, heads=heads, width=width, per=per)
    (mix,) = each(
        local_kernel,
        (queries, keys, values, decay),
        ("col", "col", "col", "dec"),
        (("col", F32),),
        flops=2 * pair_flops,
        name="local_mix",
    )
    attended, head_grad, local_reverse = each(
        norm_kernel,
        (queries, out_grad, mix, grow, query_t, incoming),
        ("col", "col", "col", "col", "row", "state"),
        (("col", BF), ("col", BF), ("state", BF)),
        flops=pair_flops // 2,
        name="norm_grad",
    )
    if chips:
        outgoing = entering_chips(local_reverse, totals, True)
    else:
        outgoing = entering((jnp.exp(total), local_reverse.astype(F32)), "seq", True)
    query_grad, key_local, value_local = each(
        back_kernel,
        (queries, keys, values, head_grad, decay, decay_t, grow, incoming),
        ("col", "col", "col", "col", "dec", "dec", "col", "state"),
        (("col", BF), ("col", F32), ("col", F32)),
        flops=6 * pair_flops,
        name="local_back",
    )
    key_grad, value_grad = each(
        close_kernel,
        (keys, values, key_local, value_local, tails, outgoing),
        ("col", "col", "col", "col", "col", "state"),
        (("col", BF), ("col", BF)),
        flops=pair_flops // 2,
        name="close_back",
    )

    span = depth // SPLIT

    def term(index, part, adds):
        return feature_term(
            (index * SPLIT + part)[None],
            key_grad,
            value_grad,
            key_weight,
            value_weight,
            adds,
            span,
        )

    up = [[] for _ in range(SPLIT)]
    down = [[] for _ in range(SPLIT)]
    for step in range(1, count):
        for part in range(SPLIT):
            if 2 * step <= count:
                index = jnp.where(
                    here < step, here + count - step, jnp.maximum(here - count + step, 0)
                )
                index = jnp.minimum(index, count - 1)
                up_send = down_send = term(index, part, up[part] + down[part])
            else:
                up_send = term(jnp.minimum(here + count - step, count - 1), part, up[part])
                down_send = term(jnp.maximum(here - count + step, 0), part, down[part])
            up[part] = [lax.ppermute(up_send, "head", scatter_pairs(count, step, True))]
            down[part] = [lax.ppermute(down_send, "head", scatter_pairs(count, step, False))]
    own = [term(here, part, []) for part in range(SPLIT)]
    feature_grad = jnp.concatenate(
        [
            (o.astype(F32) + u[0].astype(F32) + d[0].astype(F32)).astype(BF)
            for o, u, d in zip(own, up, down)
        ],
        axis=1,
    )

    norm = (tokens * blocks) ** (-0.5)
    if not chips:
        both = jnp.concatenate([key_grad, value_grad], axis=1)
        summed = lax.psum_scatter(
            lax.dot_general(gathered, both, TN, preferred_element_type=F32).astype(BF),
            "seq",
            scatter_dimension=0,
            tiled=True,
        ).astype(F32)
        summed = summed * norm
        return attended, query_grad, feature_grad, summed[:, :proj], summed[:, proj:]

    chip, core = place // 2, lax.rem(place, 2)
    out_rows = model // blocks
    turned = gathered.T.reshape(blocks // 2, 2, out_rows, tokens)
    own_t = lax.dynamic_index_in_dim(turned, core, 1, False).reshape(model // 2, tokens)
    other_t = lax.dynamic_index_in_dim(turned, 1 - core, 1, False).reshape(model // 2, tokens)
    partner_t = swap(other_t, 1)
    partner_key = swap(key_grad, 1)
    partner_value = swap(value_grad, 1)

    def block_sum(target, own_grad, partner_grad, adds, kind=BF):
        return weight_term(
            target[None], own_t, partner_t, own_grad, partner_grad, adds, out_rows, kind
        )

    outs = []
    for own_grad, partner_grad, first, second in (
        (key_grad, partner_key, 2, 4),
        (value_grad, partner_value, 4, 2),
    ):
        one, two = first // 2, second // 2
        far = swap(block_sum(chip ^ 3, own_grad, partner_grad, []), first)
        near = swap(block_sum(chip ^ one, own_grad, partner_grad, []), first)
        passed = swap(block_sum(chip ^ two, own_grad, partner_grad, [far]), second)
        mine = block_sum(chip, own_grad, partner_grad, [], F32)
        outs.append((mine + near.astype(F32) + passed.astype(F32)) * norm)
    return attended, query_grad, feature_grad, outs[0], outs[1]


def solution(mesh):
    spread = P("seq", "head")
    return jax.shard_map(
        per_device,
        mesh=mesh,
        in_specs=(spread, P(None, "head"), P(None, "head"), spread, spread, spread),
        out_specs=(spread,) * 5,
        check_vma=False,
    )
```

```python
import functools

import jax
import jax.numpy as jnp
from jax import lax
from jax.experimental import pallas as pl
from jax.experimental.pallas import tpu as pltpu
from jax.sharding import PartitionSpec as P

BF = jnp.bfloat16
F32 = jnp.float32
NT = (((1,), (1,)), ((), ()))
TN = (((0,), (0,)), ((), ()))
VMEM_LIMIT = 60 * 1024 * 1024


def dot(a, b):
    return jnp.dot(a, b, preferred_element_type=F32)


def dot_nt(a, b):
    return lax.dot_general(a, b, NT, preferred_element_type=F32)


def dot_tn(a, b):
    return lax.dot_general(a, b, TN, preferred_element_type=F32)


def params(**more):
    return pltpu.CompilerParams(vmem_limit_bytes=VMEM_LIMIT, **more)


def after(x, *done):
    return lax.optimization_barrier((x, *done))[0]


def cost(flops, data):
    return pl.CostEstimate(flops=flops, bytes_accessed=data, transcendentals=0)


def last_kv_kernel(width, pieces, index_ref, *refs):
    parts = refs[:pieces]
    kw_ref, vw_ref, ka_ref, va_ref, tail_ref, k_ref, v_ref, s_ref, held = refs[pieces:]

    @pl.when(pl.program_id(0) == 0)
    def _():
        rows = held.shape[0] // (pieces // 2)
        for i in range(pieces // 2):
            held[i * rows : (i + 1) * rows, :] = parts[2 * i][...] + parts[2 * i + 1][...]

    f = held[...]
    keys = (ka_ref[...] + dot(f, kw_ref[...])).astype(BF)
    values = (va_ref[...] + dot(f, vw_ref[...])).astype(BF)
    k_ref[...] = keys
    v_ref[...] = values
    scaled = (keys.astype(F32) * tail_ref[...]).astype(BF)
    for i in range(s_ref.shape[0]):
        cut = slice(i * width, (i + 1) * width)
        s_ref[i] = dot_tn(scaled[:, cut], values[:, cut]).astype(BF)


def last_kv(parts, index, key_weight, value_weight, key_sum, value_sum, tail, width, per):
    tokens, proj = key_sum.shape
    depth = parts[0].shape[1]
    cols = width * per
    whole = [pl.BlockSpec(p.shape, lambda j, d: (0, 0)) for p in parts]
    weight = pl.BlockSpec((depth, cols), lambda j, d: (d[0], j))
    column = pl.BlockSpec((tokens, cols), lambda j, d: (0, j))
    state = pl.BlockSpec((per, width, width), lambda j, d: (j, 0, 0))
    return pl.pallas_call(
        functools.partial(last_kv_kernel, width, len(parts)),
        grid_spec=pltpu.PrefetchScalarGridSpec(
            num_scalar_prefetch=1,
            grid=(proj // cols,),
            in_specs=whole + [weight, weight, column, column, column],
            out_specs=[column, column, state],
            scratch_shapes=[pltpu.VMEM((tokens, depth), BF)],
        ),
        out_shape=[
            jax.ShapeDtypeStruct((tokens, proj), BF),
            jax.ShapeDtypeStruct((tokens, proj), BF),
            jax.ShapeDtypeStruct((proj // width, width, width), BF),
        ],
        compiler_params=params(),
        cost_estimate=cost(4 * tokens * depth * proj, 12 * tokens * proj + 4 * depth * proj),
        name="last_kv",
    )(index, *parts, key_weight, value_weight, key_sum, value_sum, tail)


def causal_tiles(tokens):
    tile = min(256, tokens)
    for row in range(tokens // tile):
        yield slice(row * tile, (row + 1) * tile), slice(0, (row + 1) * tile)


def anti_tiles(tokens):
    tile = min(256, tokens)
    for row in range(tokens // tile):
        yield slice(row * tile, (row + 1) * tile), slice(row * tile, tokens)


def local_kernel(width, q_ref, k_ref, v_ref, dec_ref, mix_ref):
    for i in range(dec_ref.shape[0]):
        cut = slice(i * width, (i + 1) * width)
        for rows, seen in causal_tiles(q_ref.shape[0]):
            scores = dot_nt(q_ref[rows, cut], k_ref[seen, cut])
            weights = (scores * dec_ref[i, rows, seen].astype(F32)).astype(BF)
            mix_ref[rows, cut] = dot(weights, v_ref[seen, cut])


def norm_kernel(width, q_ref, g_ref, mix_ref, grow_ref, qt_ref, s_ref, att_ref, hg_ref, r_ref):
    for i in range(s_ref.shape[0]):
        cut = slice(i * width, (i + 1) * width)
        mixed = mix_ref[:, cut] + grow_ref[:, cut] * dot(q_ref[:, cut], s_ref[i])
        grad = g_ref[:, cut].astype(F32)
        scale = lax.rsqrt(jnp.mean(mixed * mixed, axis=-1, keepdims=True) + 1e-06)
        projection = jnp.mean(grad * mixed, axis=-1, keepdims=True)
        att_ref[:, cut] = (mixed * scale).astype(BF)
        head_grad = (scale * grad - mixed * (scale * scale * scale * projection)).astype(BF)
        hg_ref[:, cut] = head_grad
        r_ref[i] = dot(qt_ref[cut, :], head_grad).astype(BF)


def back_query_kernel(width, k_ref, v_ref, hg_ref, dec_ref, grow_ref, s_ref, qg_ref):
    for i in range(s_ref.shape[0]):
        cut = slice(i * width, (i + 1) * width)
        for rows, seen in causal_tiles(k_ref.shape[0]):
            pairs = dot_nt(hg_ref[rows, cut], v_ref[seen, cut])
            pairs = (pairs * dec_ref[i, rows, seen].astype(F32)).astype(BF)
            carried = grow_ref[rows, cut] * dot_nt(hg_ref[rows, cut], s_ref[i])
            qg_ref[rows, cut] = (dot(pairs, k_ref[seen, cut]) + carried).astype(BF)


def back_keys_kernel(width, q_ref, k_ref, v_ref, hg_ref, dect_ref, kg_ref, vg_ref):
    for i in range(dect_ref.shape[0]):
        cut = slice(i * width, (i + 1) * width)
        for rows, seen in anti_tiles(q_ref.shape[0]):
            decay = dect_ref[i, rows, seen].astype(F32)
            pairs = (dot_nt(v_ref[rows, cut], hg_ref[seen, cut]) * decay).astype(BF)
            kg_ref[rows, cut] = dot(pairs, q_ref[seen, cut])
            weights = (dot_nt(k_ref[rows, cut], q_ref[seen, cut]) * decay).astype(BF)
            vg_ref[rows, cut] = dot(weights, hg_ref[seen, cut])


def close_kernel(width, k_ref, v_ref, kl_ref, vl_ref, tail_ref, r_ref, grads_ref):
    for i in range(r_ref.shape[0]):
        cut = slice(i * width, (i + 1) * width)
        tail = tail_ref[:, cut]
        grads_ref[0, :, cut] = (kl_ref[:, cut] + tail * dot_nt(v_ref[:, cut], r_ref[i])).astype(BF)
        grads_ref[1, :, cut] = (vl_ref[:, cut] + tail * dot(k_ref[:, cut], r_ref[i])).astype(BF)


def per_head(kernel, args, kinds, outs, heads, width, per, flops, name):
    tokens = args[0].shape[0]
    specs = {
        "col": pl.BlockSpec((tokens, width * per), lambda j: (0, j)),
        "row": pl.BlockSpec((width * per, tokens), lambda j: (j, 0)),
        "dec": pl.BlockSpec((per, tokens, tokens), lambda j: (j, 0, 0)),
        "state": pl.BlockSpec((per, width, width), lambda j: (j, 0, 0)),
        "pair": pl.BlockSpec((2, tokens, width * per), lambda j: (0, 0, j)),
    }
    shapes = {
        "col": (tokens, heads * width),
        "state": (heads, width, width),
        "pair": (2, tokens, heads * width),
    }
    data = sum(a.size * a.dtype.itemsize for a in args)
    return pl.pallas_call(
        functools.partial(kernel, width),
        grid=(heads // per,),
        in_specs=[specs[k] for k in kinds],
        out_specs=[specs[k] for k, _ in outs],
        out_shape=[jax.ShapeDtypeStruct(shapes[k], t) for k, t in outs],
        compiler_params=params(),
        cost_estimate=cost(flops, data),
        name=name,
    )(*args)


def feature_kernel(index_ref, grads_ref, kw_ref, vw_ref, out_ref):
    total = dot_nt(grads_ref[0], kw_ref[...]) + dot_nt(grads_ref[1], vw_ref[...])
    out_ref[...] = total.astype(BF)


def feature_term(index, grads, key_weight, value_weight, span):
    _, tokens, proj = grads.shape
    tile = min(256, span)
    steps = span // tile
    weight = pl.BlockSpec((tile, proj), lambda j, d: (d[0] * steps + j, 0))
    return pl.pallas_call(
        feature_kernel,
        grid_spec=pltpu.PrefetchScalarGridSpec(
            num_scalar_prefetch=1,
            grid=(steps,),
            in_specs=[pl.BlockSpec(grads.shape, lambda j, d: (0, 0, 0)), weight, weight],
            out_specs=pl.BlockSpec((tokens, tile), lambda j, d: (0, j)),
        ),
        out_shape=jax.ShapeDtypeStruct((tokens, span), BF),
        compiler_params=params(),
        cost_estimate=cost(4 * tokens * proj * span, 4 * proj * (tokens + span)),
        name="feature_term",
    )(index[None], grads, key_weight, value_weight)


def weight_kernel(count, index_ref, fo_ref, fp_ref, go_ref, gp_ref, *refs):
    total = dot(fo_ref[0], go_ref[0]) + dot(fp_ref[0], gp_ref[0])
    for r in refs[:count]:
        total += r[...].astype(F32)
    refs[count][...] = total.astype(refs[count].dtype)


def weight_term(index, which, own_t, partner_t, grads, partner_grads, adds, kind):
    _, tokens, proj = grads.shape
    span = own_t.shape[1]
    tile = min(256, proj)
    rows = pl.BlockSpec((1, span, tokens), lambda j, d: (d[0], 0, 0))
    grad = pl.BlockSpec((1, tokens, tile), lambda j, d: (which, 0, j))
    column = pl.BlockSpec((span, tile), lambda j, d: (0, j))
    return pl.pallas_call(
        functools.partial(weight_kernel, len(adds)),
        grid_spec=pltpu.PrefetchScalarGridSpec(
            num_scalar_prefetch=1,
            grid=(proj // tile,),
            in_specs=[rows, rows, grad, grad] + [column] * len(adds),
            out_specs=column,
        ),
        out_shape=jax.ShapeDtypeStruct((span, proj), kind),
        compiler_params=params(),
        cost_estimate=cost(4 * tokens * proj * span, 4 * tokens * (proj + span)),
        name="weight_term",
    )(index[None], own_t, partner_t, grads, partner_grads, *adds)


def turn_kernel(count, info_ref, *refs):
    shards, (own_ref, other_ref, held, turned, sem) = refs[: 2 * count - 1], refs[2 * count - 1 :]
    relative = pl.program_id(0) - info_ref[0]
    core = info_ref[1]
    for i, shard in enumerate(shards):
        offset = i if i < count else count - 1 - i

        @pl.when(relative == offset)
        def _():
            copy = pltpu.make_async_copy(shard, held, sem)
            copy.start()
            copy.wait()

    turned[...] = held[...].T
    rows = own_ref.shape[1]
    own_ref[0] = turned[pl.ds(pl.multiple_of(core * rows, rows), rows), :]
    other_ref[0] = turned[pl.ds(pl.multiple_of((1 - core) * rows, rows), rows), :]


def turn_features(info, shards, count):
    tokens, depth = shards[0].shape
    half = pl.BlockSpec((1, depth // 2, tokens), lambda j, d: (j, 0, 0))
    return pl.pallas_call(
        functools.partial(turn_kernel, count),
        grid_spec=pltpu.PrefetchScalarGridSpec(
            num_scalar_prefetch=1,
            grid=(count,),
            in_specs=[pl.BlockSpec(memory_space=pl.ANY)] * len(shards),
            out_specs=[half, half],
            scratch_shapes=[
                pltpu.VMEM((tokens, depth), BF),
                pltpu.VMEM((depth, tokens), BF),
                pltpu.SemaphoreType.DMA,
            ],
        ),
        out_shape=[jax.ShapeDtypeStruct((count, depth // 2, tokens), BF)] * 2,
        compiler_params=params(),
        cost_estimate=cost(0, 16 * tokens * depth * count),
        name="turn_features",
    )(info, *shards)


def merge_states(earlier, later):
    return (earlier[0] * later[0], later[0][:, None, None] * earlier[1] + later[1])


def entering(x, axis, backward):
    count = lax.axis_size(axis)
    place = lax.axis_index(axis)
    ahead = count - 1 - place if backward else place
    gathered = tuple(lax.all_gather(a.astype(BF), axis) for a in x)
    state = (jnp.ones_like(x[0]), jnp.zeros_like(x[1]))

    def one(hop, state):
        source = count - 1 - hop if backward else hop
        item = tuple(
            lax.dynamic_index_in_dim(a, source, 0, False).astype(own.dtype)
            for a, own in zip(gathered, x)
        )
        return merge_states(state, item)

    return lax.fori_loop(0, ahead, one, state)[1].astype(BF)


def swap(x, bit, keep=None):
    pairs = [(s, s ^ bit) for s in range(8) if keep is None or keep(s)]
    return lax.ppermute(x, "seq", pairs)


def gather_totals(own):
    place = lax.axis_index("seq")
    held = own[None]
    for bit in (1, 2, 4):
        other = swap(held, bit)
        upper = (place & bit) != 0
        held = jnp.concatenate(
            [jnp.where(upper, other, held), jnp.where(upper, held, other)], axis=0
        )
    return held


def entering_chips(state, totals, backward, first_wait, second_wait):
    place = lax.axis_index("seq")
    core = lax.rem(place, 2)
    half = state.shape[0] // 2
    ahead_of = (lambda bit: (place & bit) == 0) if backward else (lambda bit: (place & bit) != 0)
    decay = jnp.exp(totals)[:, :, None, None]

    def halves(a):
        return lax.dynamic_slice_in_dim(a, core * half, half, 0)

    def join(own, other, bit, own_factor, other_factor):
        late = ahead_of(bit)
        own, other = own.astype(F32), other.astype(F32)
        return jnp.where(late, own_factor * other + own, other_factor * own + other)

    partner = swap(state, 1)
    own_decay, partner_decay = decay[place], decay[place ^ 1]
    chip = join(halves(state), halves(partner), 1, halves(own_decay), halves(partner_decay)).astype(BF)
    beside = after(swap(chip, 2), *first_wait)
    chip_decay = halves(own_decay * partner_decay)
    beside_decay = halves(decay[place ^ 2] * decay[place ^ 3])
    pair = join(chip, beside, 2, chip_decay, beside_decay).astype(BF)
    keep = (lambda s: (s & 4) != 0) if backward else (lambda s: (s & 4) == 0)
    passed = after(swap(pair, 4, keep), *second_wait).astype(F32)
    entered = jnp.where(ahead_of(2), beside_decay * passed + beside.astype(F32), passed).astype(BF)
    other = swap(entered, 1)
    whole = jnp.where(
        core == 0, jnp.concatenate([entered, other]), jnp.concatenate([other, entered])
    )
    step = partner_decay * whole.astype(F32) + partner.astype(F32)
    return jnp.where(ahead_of(1), step.astype(BF), whole)


def line_pairs(count, step, up):
    if up:
        return [(i, i + 1) for i in range(step - 1, count - 1)]
    return [(i, i - 1) for i in range(1, count - step + 1)]


def scatter_pairs(count, step, up):
    if up:
        return [(i, i + 1) for i in range(0, min(step, count - 1))]
    return [(i, i - 1) for i in range(max(1, count - step), count)]


def per_device(features, key_weight, value_weight, queries, log_decay, out_grad):
    tokens, proj = queries.shape
    depth = features.shape[1]
    model = key_weight.shape[0]
    heads = log_decay.shape[1]
    width = proj // heads
    per = 2 if heads % 2 == 0 else 1
    count = lax.axis_size("head")
    blocks = lax.axis_size("seq")
    here = lax.axis_index("head")
    place = lax.axis_index("seq")
    chips = blocks == 8 and model == 8 * 512 and count == 4

    cum = jnp.cumsum(log_decay, axis=0)
    total = cum[-1]
    growth = jnp.exp(cum)
    tail = jnp.exp(total[None, :] - cum)
    grow = jnp.repeat(growth, width, axis=1)
    tails = jnp.repeat(tail, width, axis=1)
    positions = jnp.arange(tokens)
    causal = (positions[:, None] >= positions[None, :])[None]
    cum_t = cum.T
    gap = cum_t[:, :, None] - cum_t[:, None, :]
    decay = jnp.where(causal, jnp.exp(jnp.where(causal, gap, 0.0)), 0.0).astype(BF)
    causal_t = (positions[:, None] <= positions[None, :])[None]
    decay_t = jnp.where(causal_t, jnp.exp(jnp.where(causal_t, -gap, 0.0)), 0.0).astype(BF)
    query_t = (queries.astype(F32) * grow).astype(BF).T

    up = down = features
    ups, downs = [], []

    def rows_of(weight, index):
        return lax.dynamic_slice_in_dim(weight, index * depth, depth, 0)

    key_sum = dot(features, rows_of(key_weight, here))
    value_sum = dot(features, rows_of(value_weight, here))
    for step in range(1, count):
        up = lax.ppermute(up, "head", line_pairs(count, step, True))
        down = lax.ppermute(down, "head", line_pairs(count, step, False))
        ups.append(up)
        downs.append(down)
        if 2 * step >= count:
            index = jnp.where(here >= step, here - step, jnp.minimum(here + step, count - 1))
            shards = [(up + down, index)]
        else:
            shards = [
                (up, jnp.maximum(here - step, 0)),
                (down, jnp.minimum(here + step, count - 1)),
            ]
        if step < count - 1:
            for shard, index in shards:
                key_sum = key_sum + dot(shard, rows_of(key_weight, index))
                value_sum = value_sum + dot(shard, rows_of(value_weight, index))
    totals = gather_totals(total) if chips else total
    key_sum = after(key_sum, totals, decay, decay_t, query_t, grow, tails)
    keys, values, local_state = last_kv(
        (up, down), index[None], key_weight, value_weight, key_sum, value_sum, tails, width, per
    )

    pair_flops = 2 * heads * tokens * tokens * width
    each = functools.partial(per_head, heads=heads, width=width, per=per)
    (mix,) = each(
        local_kernel,
        (queries, keys, values, decay),
        ("col", "col", "col", "dec"),
        (("col", F32),),
        flops=2 * pair_flops,
        name="local_mix",
    )
    if chips:
        chip, core = place // 2, lax.rem(place, 2)
        own_t, other_t = turn_features(jnp.stack([here, core]), (features, *downs, *ups), count)
        incoming = entering_chips(local_state, totals, False, (mix,), (own_t,))
        partner_t = swap(other_t, 1)
    else:
        incoming = entering((jnp.exp(total), local_state.astype(F32)), "seq", False)
    attended, head_grad, local_reverse = each(
        norm_kernel,
        (queries, out_grad, mix, grow, query_t, incoming),
        ("col", "col", "col", "col", "row", "state"),
        (("col", BF), ("col", BF), ("state", BF)),
        flops=pair_flops // 2,
        name="norm_grad",
    )
    (query_grad,) = each(
        back_query_kernel,
        (keys, values, head_grad, decay, grow, incoming),
        ("col", "col", "col", "dec", "col", "state"),
        (("col", BF),),
        flops=2 * pair_flops,
        name="back_query",
    )
    key_local, value_local = each(
        back_keys_kernel,
        (queries, keys, values, head_grad, decay_t),
        ("col", "col", "col", "col", "dec"),
        (("col", F32), ("col", F32)),
        flops=4 * pair_flops,
        name="back_keys",
    )
    if chips:
        outgoing = entering_chips(local_reverse, totals, True, (query_grad,), (key_local,))
    else:
        outgoing = entering((jnp.exp(total), local_reverse.astype(F32)), "seq", True)
    (grads,) = each(
        close_kernel,
        (keys, values, key_local, value_local, tails, outgoing),
        ("col", "col", "col", "col", "col", "state"),
        (("pair", BF),),
        flops=pair_flops // 2,
        name="close_back",
    )

    def term(index, done):
        return feature_term(after(index, *done), grads, key_weight, value_weight, depth)

    def add(*terms):
        return sum(t.astype(F32) for t in terms).astype(BF)

    def scatter_indices(step):
        upward = jnp.minimum(here + count - step, count - 1)
        downward = jnp.maximum(here - count + step, 0)
        return upward, downward, jnp.where(here < step, upward, downward)

    def send(step, up_sum, down_sum):
        return (
            lax.ppermute(up_sum, "head", scatter_pairs(count, step, True)),
            lax.ppermute(down_sum, "head", scatter_pairs(count, step, False)),
        )

    def feature_step(step, up, down, done):
        upward, downward, either = scatter_indices(step)
        if 2 * step <= count:
            own = term(either, done)
            total = own if up is None else add(own, up, down)
            return send(step, total, total), total
        own_up = term(upward, done)
        own_down = term(downward, (own_up,))
        up_sum = add(own_up, up)
        return send(step, up_sum, add(own_down, down)), own_down

    norm = (tokens * blocks) ** (-0.5)
    if not chips:
        up = down = None
        done = (grads,)
        for step in range(1, count):
            (up, down), last = feature_step(step, up, down, done)
            done = (last,)
        feature_grad = add(term(here, done), up, down)
        gathered = lax.all_gather(features, "head", axis=1, tiled=True)
        both = jnp.concatenate([grads[0], grads[1]], axis=1)
        summed = lax.psum_scatter(
            lax.dot_general(gathered, both, TN, preferred_element_type=F32).astype(BF),
            "seq",
            scatter_dimension=0,
            tiled=True,
        ).astype(F32)
        summed = summed * norm
        return attended, query_grad, feature_grad, summed[:, :proj], summed[:, proj:]

    partner_grads = swap(grads, 1)

    def block(target, which, adds, done, kind=BF):
        return weight_term(
            after(target, *done), which, own_t, partner_t, grads, partner_grads, adds, kind
        )

    (up, down), last = feature_step(1, None, None, (grads,))
    key_far = block(chip ^ 3, 0, [], (last,))
    value_far = block(chip ^ 3, 1, [], (key_far,))
    key_near = block(chip ^ 1, 0, [], (value_far,))
    value_near = block(chip ^ 2, 1, [], (key_near,))
    got_key_far, got_value_far = swap(key_far, 2), swap(value_far, 4)
    got_key_near, got_value_near = swap(key_near, 2), swap(value_near, 4)
    (up, down), last = feature_step(2, up, down, (value_near,))
    key_pass = block(chip ^ 2, 0, [got_key_far], (last,))
    value_pass = block(chip ^ 1, 1, [got_value_far], (key_pass,))
    got_key, got_value = swap(key_pass, 4), swap(value_pass, 2)
    (up, down), last = feature_step(3, up, down, (value_pass,))
    feature_own = term(here, (last,))
    key_own = block(chip, 0, [], (feature_own,), F32)
    value_own = block(chip, 1, [], (key_own,), F32)
    feature_grad = add(feature_own, up, down)
    key_out = (key_own + got_key_near.astype(F32) + got_key.astype(F32)) * norm
    value_out = (value_own + got_value_near.astype(F32) + got_value.astype(F32)) * norm
    return attended, query_grad, feature_grad, key_out, value_out


def solution(mesh):
    spread = P("seq", "head")
    return jax.shard_map(
        per_device,
        mesh=mesh,
        in_specs=(spread, P(None, "head"), P(None, "head"), spread, spread, spread),
        out_specs=(spread,) * 5,
        check_vma=False,
    )
```

```python
import functools

import jax
import jax.numpy as jnp
from jax import lax
from jax.experimental import pallas as pl
from jax.experimental.pallas import tpu as pltpu
from jax.sharding import PartitionSpec as P

BF = jnp.bfloat16
F32 = jnp.float32
NT = (((1,), (1,)), ((), ()))
TN = (((0,), (0,)), ((), ()))
MIB = 1024 * 1024


def dot(a, b):
    return jnp.dot(a, b, preferred_element_type=F32)


def dot_nt(a, b):
    return lax.dot_general(a, b, NT, preferred_element_type=F32)


def dot_tn(a, b):
    return lax.dot_general(a, b, TN, preferred_element_type=F32)


def params(limit=16):
    return pltpu.CompilerParams(vmem_limit_bytes=limit * MIB)


def after(x, *done):
    return lax.optimization_barrier((x, *done))[0]


def after_all(*arrays):
    return lax.optimization_barrier(arrays)


SMALL = pl.CostEstimate(flops=1, bytes_accessed=1, transcendentals=0)


def tiles(tokens, causal):
    tile = min(256, tokens)
    for row in range(tokens // tile):
        first, last = row * tile, (row + 1) * tile
        yield slice(first, last), slice(0, last) if causal else slice(first, tokens)


def column(cum_ref, head):
    lanes = lax.broadcasted_iota(jnp.int32, cum_ref.shape, 1)
    return jnp.sum(jnp.where(lanes == head, cum_ref[...], 0.0), axis=1, keepdims=True)


def decay_tile(across, down, rows, seen, causal):
    shape = (rows.stop - rows.start, seen.stop - seen.start)
    one = rows.start + lax.broadcasted_iota(jnp.int32, shape, 0)
    two = seen.start + lax.broadcasted_iota(jnp.int32, shape, 1)
    gap = down[rows] - across[:, seen]
    if causal:
        return jnp.where(two <= one, jnp.exp(gap), 0.0)
    return jnp.where(one <= two, jnp.exp(-gap), 0.0)


def heads_of(per, width):
    for i in range(per):
        yield i, pl.program_id(0) * per + i, slice(i * width, (i + 1) * width)


def state_kernel(width, per, cum_ref, k_ref, v_ref, s_ref):
    for i, head, cut in heads_of(per, width):
        down = column(cum_ref, head)
        tail = jnp.exp(down[-1:] - down)
        scaled = (k_ref[:, cut].astype(F32) * tail).astype(BF)
        s_ref[i] = dot_tn(scaled, v_ref[:, cut]).astype(BF)


def local_kernel(width, per, cum_ref, cumt_ref, q_ref, k_ref, v_ref, mix_ref):
    for i, head, cut in heads_of(per, width):
        down, across = column(cum_ref, head), cumt_ref[pl.ds(head, 1), :]
        for rows, seen in tiles(q_ref.shape[0], True):
            scores = dot_nt(q_ref[rows, cut], k_ref[seen, cut])
            weights = (scores * decay_tile(across, down, rows, seen, True)).astype(BF)
            mix_ref[rows, cut] = dot(weights, v_ref[seen, cut]).astype(mix_ref.dtype)


def norm_kernel(width, per, cum_ref, q_ref, g_ref, mix_ref, s_ref, att_ref, hg_ref, r_ref):
    for i, head, cut in heads_of(per, width):
        grow = jnp.exp(column(cum_ref, head))
        carried = grow * dot(q_ref[:, cut], s_ref[i])
        mixed = mix_ref[:, cut].astype(F32) + carried
        grad = g_ref[:, cut].astype(F32)
        scale = lax.rsqrt(jnp.mean(mixed * mixed, axis=-1, keepdims=True) + 1e-06)
        projection = jnp.mean(grad * mixed, axis=-1, keepdims=True)
        att_ref[:, cut] = (mixed * scale).astype(BF)
        head_grad = (scale * grad - mixed * (scale * scale * scale * projection)).astype(BF)
        hg_ref[:, cut] = head_grad
        grown = (q_ref[:, cut].astype(F32) * grow).astype(BF)
        r_ref[i] = dot_tn(grown, head_grad).astype(BF)


def back_query_kernel(width, per, cum_ref, cumt_ref, k_ref, v_ref, hg_ref, s_ref, qg_ref):
    for i, head, cut in heads_of(per, width):
        down, across = column(cum_ref, head), cumt_ref[pl.ds(head, 1), :]
        grow = jnp.exp(down)
        for rows, seen in tiles(k_ref.shape[0], True):
            pairs = dot_nt(hg_ref[rows, cut], v_ref[seen, cut])
            pairs = (pairs * decay_tile(across, down, rows, seen, True)).astype(BF)
            carried = grow[rows] * dot_nt(hg_ref[rows, cut], s_ref[i])
            qg_ref[rows, cut] = (dot(pairs, k_ref[seen, cut]) + carried).astype(BF)


def back_keys_kernel(width, per, cum_ref, cumt_ref, q_ref, k_ref, v_ref, hg_ref, kg_ref, vg_ref):
    for i, head, cut in heads_of(per, width):
        down, across = column(cum_ref, head), cumt_ref[pl.ds(head, 1), :]
        for rows, seen in tiles(q_ref.shape[0], False):
            decay = decay_tile(across, down, rows, seen, False)
            pairs = (dot_nt(v_ref[rows, cut], hg_ref[seen, cut]) * decay).astype(BF)
            kg_ref[rows, cut] = dot(pairs, q_ref[seen, cut]).astype(kg_ref.dtype)
            weights = (dot_nt(k_ref[rows, cut], q_ref[seen, cut]) * decay).astype(BF)
            vg_ref[rows, cut] = dot(weights, hg_ref[seen, cut]).astype(vg_ref.dtype)


def close_kernel(width, per, cum_ref, k_ref, v_ref, kl_ref, vl_ref, r_ref, kg_ref, vg_ref):
    for i, head, cut in heads_of(per, width):
        down = column(cum_ref, head)
        tail = jnp.exp(down[-1:] - down)
        key_carried = tail * dot_nt(v_ref[:, cut], r_ref[i])
        value_carried = tail * dot(k_ref[:, cut], r_ref[i])
        kg_ref[:, cut] = (kl_ref[:, cut].astype(F32) + key_carried).astype(BF)
        vg_ref[:, cut] = (vl_ref[:, cut].astype(F32) + value_carried).astype(BF)


def per_head(kernel, args, kinds, outs, tokens, heads, width, per, name, limit=60):
    specs = {
        "cum": pl.BlockSpec((tokens, heads), lambda j: (0, 0)),
        "cumt": pl.BlockSpec((heads, tokens), lambda j: (0, 0)),
        "col": pl.BlockSpec((tokens, width * per), lambda j: (0, j)),
        "state": pl.BlockSpec((per, width, width), lambda j: (j, 0, 0)),
    }
    shapes = {"col": (tokens, heads * width), "state": (heads, width, width)}
    return pl.pallas_call(
        functools.partial(kernel, width, per),
        grid=(heads // per,),
        in_specs=[specs[k] for k in kinds],
        out_specs=[specs[k] for k in outs],
        out_shape=[jax.ShapeDtypeStruct(shapes[k], BF) for k in outs],
        compiler_params=params(limit),
        cost_estimate=SMALL,
        name=name,
    )(*args)


def feature_kernel(count, index_ref, kg_ref, vg_ref, kw_ref, vw_ref, *refs):
    total = dot_nt(kg_ref[...], kw_ref[...]) + dot_nt(vg_ref[...], vw_ref[...])
    for r in refs[:count]:
        total += r[...].astype(F32)
    refs[count][0] = total.astype(BF)


def feature_terms(indices, key_grad, value_grad, key_weight, value_weight, adds, span):
    tokens, proj = key_grad.shape
    tile = min(512, span)
    steps = span // tile
    whole = pl.BlockSpec((tokens, proj), lambda i, j, d: (0, 0))
    weight = pl.BlockSpec((tile, proj), lambda i, j, d: (d[i] * steps + j, 0))
    number = indices.shape[0]
    return pl.pallas_call(
        functools.partial(feature_kernel, len(adds)),
        grid_spec=pltpu.PrefetchScalarGridSpec(
            num_scalar_prefetch=1,
            grid=(number, steps),
            in_specs=[whole, whole, weight, weight]
            + [pl.BlockSpec((tokens, tile), lambda i, j, d: (0, j))] * len(adds),
            out_specs=pl.BlockSpec((1, tokens, tile), lambda i, j, d: (i, 0, j)),
        ),
        out_shape=jax.ShapeDtypeStruct((number, tokens, span), BF),
        compiler_params=params(60),
        cost_estimate=SMALL,
        name="feature_terms",
    )(indices, key_grad, value_grad, key_weight, value_weight, *adds)


def weight_kernel(index_ref, fo_ref, fp_ref, go_ref, gp_ref, out_ref):
    total = dot(fo_ref[0], go_ref[...]) + dot(fp_ref[0], gp_ref[...])
    out_ref[0] = total.astype(out_ref.dtype)


def weight_terms(slots, own_t, partner_t, grad, partner_grad, kind):
    tokens, proj = grad.shape
    span = own_t.shape[1]
    number = slots.shape[0]
    tile = min(512, proj)
    rows = pl.BlockSpec((1, span, tokens), lambda j, i, d: (d[i], 0, 0))
    cols = pl.BlockSpec((tokens, tile), lambda j, i, d: (0, j))
    return pl.pallas_call(
        weight_kernel,
        grid_spec=pltpu.PrefetchScalarGridSpec(
            num_scalar_prefetch=1,
            grid=(proj // tile, number),
            in_specs=[rows, rows, cols, cols],
            out_specs=pl.BlockSpec((1, span, tile), lambda j, i, d: (i, 0, j)),
        ),
        out_shape=jax.ShapeDtypeStruct((number, span, proj), kind),
        compiler_params=params(60),
        cost_estimate=SMALL,
        name="weight_terms",
    )(slots, own_t, partner_t, grad, partner_grad)


def turn_kernel(aliased, core_ref, *refs):
    shards, (own_ref, other_ref, held, turned, sem) = refs[aliased:-5], refs[-5:]
    core = core_ref[0]
    for i, shard in enumerate(shards):

        @pl.when(pl.program_id(0) == i)
        def _():
            copy = pltpu.make_async_copy(shard, held, sem)
            copy.start()
            copy.wait()

    turned[...] = held[...].T
    rows = own_ref.shape[1]
    own_ref[0] = turned[pl.ds(pl.multiple_of(core * rows, rows), rows), :]
    other_ref[0] = turned[pl.ds(pl.multiple_of((1 - core) * rows, rows), rows), :]


def turn_features(core, shards, first, slots, held=()):
    tokens, depth = shards[0].shape
    half = pl.BlockSpec((1, depth // 2, tokens), lambda j, d: (first + j, 0, 0))
    aliased = len(held)
    return pl.pallas_call(
        functools.partial(turn_kernel, aliased),
        grid_spec=pltpu.PrefetchScalarGridSpec(
            num_scalar_prefetch=1,
            grid=(len(shards),),
            in_specs=[pl.BlockSpec(memory_space=pl.ANY)] * (aliased + len(shards)),
            out_specs=[half, half],
            scratch_shapes=[
                pltpu.VMEM((tokens, depth), BF),
                pltpu.VMEM((depth, tokens), BF),
                pltpu.SemaphoreType.DMA,
            ],
        ),
        out_shape=[jax.ShapeDtypeStruct((slots, depth // 2, tokens), BF)] * 2,
        input_output_aliases={1 + i: i for i in range(aliased)},
        compiler_params=params(),
        cost_estimate=SMALL,
        name="turn_features",
    )(core[None], *held, *shards)


def merge_states(earlier, later):
    return (earlier[0] * later[0], later[0][:, None, None] * earlier[1] + later[1])


def entering(x, axis, backward):
    count = lax.axis_size(axis)
    place = lax.axis_index(axis)
    ahead = count - 1 - place if backward else place
    gathered = tuple(lax.all_gather(a.astype(BF), axis) for a in x)
    state = (jnp.ones_like(x[0]), jnp.zeros_like(x[1]))

    def one(hop, state):
        source = count - 1 - hop if backward else hop
        item = tuple(
            lax.dynamic_index_in_dim(a, source, 0, False).astype(own.dtype)
            for a, own in zip(gathered, x)
        )
        return merge_states(state, item)

    return lax.fori_loop(0, ahead, one, state)[1].astype(BF)


def swap(x, bit, keep=None):
    pairs = [(s, s ^ bit) for s in range(8) if keep is None or keep(s)]
    return lax.ppermute(x, "seq", pairs)


def gather_totals(own):
    place = lax.axis_index("seq")
    held = own[None]
    for bit in (1, 2, 4):
        other = swap(held, bit)
        upper = (place & bit) != 0
        held = jnp.concatenate(
            [jnp.where(upper, other, held), jnp.where(upper, held, other)], axis=0
        )
    return held


def entering_chips(state, totals, backward, first_wait, second_wait):
    place = lax.axis_index("seq")
    core = lax.rem(place, 2)
    half = state.shape[0] // 2
    ahead_of = (lambda bit: (place & bit) == 0) if backward else (lambda bit: (place & bit) != 0)
    decay = jnp.exp(totals)[:, :, None, None]

    def halves(a):
        return lax.dynamic_slice_in_dim(a, core * half, half, 0)

    def join(own, other, bit, own_factor, other_factor):
        late = ahead_of(bit)
        own, other = own.astype(F32), other.astype(F32)
        return jnp.where(late, own_factor * other + own, other_factor * own + other)

    partner = swap(state, 1)
    own_decay, partner_decay = decay[place], decay[place ^ 1]
    chip = join(halves(state), halves(partner), 1, halves(own_decay), halves(partner_decay)).astype(BF)
    beside = after(swap(chip, 2), *first_wait)
    chip_decay = halves(own_decay * partner_decay)
    beside_decay = halves(decay[place ^ 2] * decay[place ^ 3])
    pair = join(chip, beside, 2, chip_decay, beside_decay).astype(BF)
    keep = (lambda s: (s & 4) != 0) if backward else (lambda s: (s & 4) == 0)
    passed = after(swap(pair, 4, keep), *second_wait).astype(F32)
    entered = jnp.where(ahead_of(2), beside_decay * passed + beside.astype(F32), passed).astype(BF)
    other = swap(entered, 1)
    whole = jnp.where(
        core == 0, jnp.concatenate([entered, other]), jnp.concatenate([other, entered])
    )
    step = partner_decay * whole.astype(F32) + partner.astype(F32)
    return jnp.where(ahead_of(1), step.astype(BF), whole)


def line_pairs(count, step, up):
    if up:
        return [(i, i + 1) for i in range(step - 1, count - 1)]
    return [(i, i - 1) for i in range(1, count - step + 1)]


def scatter_pairs(count, step, up):
    if up:
        return [(i, i + 1) for i in range(0, min(step, count - 1))]
    return [(i, i - 1) for i in range(max(1, count - step), count)]


def per_device(features, key_weight, value_weight, queries, log_decay, out_grad):
    tokens, proj = queries.shape
    depth = features.shape[1]
    model = key_weight.shape[0]
    heads = log_decay.shape[1]
    width = proj // heads
    per = 2 if heads % 2 == 0 else 1
    count = lax.axis_size("head")
    blocks = lax.axis_size("seq")
    here = lax.axis_index("head")
    place = lax.axis_index("seq")
    chips = blocks == 8 and model == 8 * 512 and count == 4

    cum = jnp.cumsum(log_decay, axis=0)
    cum_t = cum.T
    total = cum[-1]

    up = down = features

    def rows_of(weight, index):
        return lax.dynamic_slice_in_dim(weight, index * depth, depth, 0)

    def project(sums, shard, index):
        key_part = dot(shard, rows_of(key_weight, index))
        value_part = dot(shard, rows_of(value_weight, index))
        return [key_part, value_part] if sums is None else [sums[0] + key_part, sums[1] + value_part]

    if chips:
        core = lax.rem(place, 2)
        totals = gather_totals(total)
    sums = project(None, features, here)
    slots = [features]
    turned = ()
    for step in range(1, count):
        up = lax.ppermute(up, "head", line_pairs(count, step, True))
        down = lax.ppermute(down, "head", line_pairs(count, step, False))
        if chips and step == count - 2:
            turned = turn_features(core, slots, 0, 5)
            up, down, sums, turned, totals = after_all(up, down, sums, turned, totals)
        else:
            up, down, sums = after_all(up, down, sums)
        if 2 * step >= count:
            index = jnp.where(here >= step, here - step, jnp.minimum(here + step, count - 1))
            shards = [(up + down, index)]
        else:
            shards = [
                (down, jnp.minimum(here + step, count - 1)),
                (up, jnp.maximum(here - step, 0)),
            ]
        slots += [shard for shard, _ in shards]
        for shard, index in shards:
            sums = project(sums, shard, index)
    key_sum, value_sum = sums
    keys, values = key_sum.astype(BF), value_sum.astype(BF)

    each = functools.partial(per_head, tokens=tokens, heads=heads, width=width, per=per)
    (local_state,) = each(
        state_kernel,
        (cum, keys, values),
        ("cum", "col", "col"),
        ("state",),
        name="local_state",
        limit=16,
    )
    (mix,) = each(
        local_kernel,
        (cum, cum_t, queries, keys, values),
        ("cum", "cumt", "col", "col", "col"),
        ("col",),
        name="local_mix",
    )
    if chips:
        own_t, other_t = turn_features(core, slots[3:], 3, 5, turned)
        partner_t = swap(other_t, 1)
        incoming = entering_chips(local_state, totals, False, (mix,), (own_t,))
    else:
        incoming = entering((jnp.exp(total), local_state.astype(F32)), "seq", False)
    attended, head_grad, local_reverse = each(
        norm_kernel,
        (cum, queries, out_grad, mix, incoming),
        ("cum", "col", "col", "col", "state"),
        ("col", "col", "state"),
        name="norm_grad",
    )
    (query_grad,) = each(
        back_query_kernel,
        (cum, cum_t, keys, values, head_grad, incoming),
        ("cum", "cumt", "col", "col", "col", "state"),
        ("col",),
        name="back_query",
    )
    key_local, value_local = each(
        back_keys_kernel,
        (cum, cum_t, queries, keys, values, head_grad),
        ("cum", "cumt", "col", "col", "col", "col"),
        ("col", "col"),
        name="back_keys",
    )
    if chips:
        outgoing = entering_chips(local_reverse, totals, True, (query_grad,), (key_local,))
    else:
        outgoing = entering((jnp.exp(total), local_reverse.astype(F32)), "seq", True)
    key_grad, value_grad = each(
        close_kernel,
        (cum, keys, values, key_local, value_local, outgoing),
        ("cum", "col", "col", "col", "col", "state"),
        ("col", "col"),
        name="close_back",
    )

    def terms(indices, done, adds=()):
        indices = after(jnp.stack(indices), *done)
        return feature_terms(indices, key_grad, value_grad, key_weight, value_weight, adds, depth)

    def add(*terms):
        return sum(t.astype(F32) for t in terms).astype(BF)

    def scatter_indices(step):
        upward = jnp.minimum(here + count - step, count - 1)
        downward = jnp.maximum(here - count + step, 0)
        return upward, downward, jnp.where(here < step, upward, downward)

    def send(step, up_sum, down_sum):
        return (
            lax.ppermute(up_sum, "head", scatter_pairs(count, step, True)),
            lax.ppermute(down_sum, "head", scatter_pairs(count, step, False)),
        )

    def feature_step(step, up, down, done):
        upward, downward, either = scatter_indices(step)
        if 2 * step <= count:
            total = terms([either], done, () if up is None else (up, down))[0]
            return send(step, total, total), total
        both = terms([upward, downward], done)
        return send(step, add(both[0], up), add(both[1], down)), both

    norm = (tokens * blocks) ** (-0.5)
    if not chips:
        up = down = None
        done = (key_grad,)
        for step in range(1, count):
            (up, down), last = feature_step(step, up, down, done)
            done = (last,)
        feature_grad = terms([here], done, (up, down))[0]
        gathered = lax.all_gather(features, "head", axis=1, tiled=True)
        both = jnp.concatenate([key_grad, value_grad], axis=1)
        summed = lax.psum_scatter(
            lax.dot_general(gathered, both, TN, preferred_element_type=F32).astype(BF),
            "seq",
            scatter_dimension=0,
            tiled=True,
        ).astype(F32)
        summed = summed * norm
        return attended, query_grad, feature_grad, summed[:, :proj], summed[:, proj:]

    chip = place // 2
    pairs = [(g, swap(g, 1)) for g in (key_grad, value_grad)]

    def blocks_for(targets, which, done, kind=BF):
        offset = after(jnp.stack(targets), *done) - here
        far = jnp.abs(offset)
        slot = jnp.where(far < 2, jnp.where(offset < 0, 2, far), far + 1)
        return weight_terms(slot, own_t, partner_t, *pairs[which], kind)

    (up, down), last = feature_step(1, None, None, (key_grad,))
    key_away = blocks_for([chip ^ 3, chip ^ 1], 0, (last,))
    got_key = swap(key_away, 2)
    value_away = blocks_for([chip ^ 3, chip ^ 2], 1, (key_away,))
    got_value = swap(value_away, 4)
    upward, downward, either = scatter_indices(2)
    last = terms([either], (value_away,))[0]
    total = add(last, up, down)
    up, down = send(2, total, total)
    upward, downward, _ = scatter_indices(3)
    feature_up, feature_down, feature_own = last = terms([upward, downward, here], (total,))
    key_pass = blocks_for([chip ^ 2], 0, (last,))
    value_pass = blocks_for([chip ^ 1], 1, (key_pass,))
    key_own = blocks_for([chip], 0, (value_pass,), F32)[0]
    value_own = blocks_for([chip], 1, (key_own,), F32)[0]
    up = after(up, value_own)
    up, down = send(3, add(feature_up, up), add(feature_down, down))
    key_passed = swap(add(key_pass[0], got_key[0]), 4)
    value_passed = swap(add(value_pass[0], got_value[0]), 2)
    feature_grad = add(feature_own, up, down)
    key_out = (key_own + got_key[1].astype(F32) + key_passed.astype(F32)) * norm
    value_out = (value_own + got_value[1].astype(F32) + value_passed.astype(F32)) * norm
    return attended, query_grad, feature_grad, key_out, value_out


def solution(mesh):
    spread = P("seq", "head")
    return jax.shard_map(
        per_device,
        mesh=mesh,
        in_specs=(spread, P(None, "head"), P(None, "head"), spread, spread, spread),
        out_specs=(spread,) * 5,
        check_vma=False,
    )
```

```python
import functools

import jax
import jax.numpy as jnp
from jax import lax
from jax.experimental import pallas as pl
from jax.experimental.pallas import tpu as pltpu
from jax.sharding import PartitionSpec as P

BF = jnp.bfloat16
F32 = jnp.float32
NT = (((1,), (1,)), ((), ()))
TN = (((0,), (0,)), ((), ()))
MIB = 1024 * 1024


def dot(a, b):
    return jnp.dot(a, b, preferred_element_type=F32)


def dot_nt(a, b):
    return lax.dot_general(a, b, NT, preferred_element_type=F32)


def dot_tn(a, b):
    return lax.dot_general(a, b, TN, preferred_element_type=F32)


def params(limit=16):
    return pltpu.CompilerParams(vmem_limit_bytes=limit * MIB)


def together(*arrays):
    return lax.optimization_barrier(arrays)


SMALL = pl.CostEstimate(flops=1, bytes_accessed=1, transcendentals=0)


def tiles(tokens, causal):
    tile = min(256, tokens)
    for row in range(tokens // tile):
        first, last = row * tile, (row + 1) * tile
        yield slice(first, last), slice(0, last) if causal else slice(first, tokens)


def column(cum_ref, head):
    lanes = lax.broadcasted_iota(jnp.int32, cum_ref.shape, 1)
    return jnp.sum(jnp.where(lanes == head, cum_ref[...], 0.0), axis=1, keepdims=True)


def decay_tile(across, down, rows, seen, causal):
    shape = (rows.stop - rows.start, seen.stop - seen.start)
    one = rows.start + lax.broadcasted_iota(jnp.int32, shape, 0)
    two = seen.start + lax.broadcasted_iota(jnp.int32, shape, 1)
    gap = down[rows] - across[:, seen]
    if causal:
        return jnp.where(two <= one, jnp.exp(gap), 0.0)
    return jnp.where(one <= two, jnp.exp(-gap), 0.0)


def heads_of(per, width):
    for i in range(per):
        yield i, pl.program_id(0) * per + i, slice(i * width, (i + 1) * width)


def state_kernel(width, per, cum_ref, k_ref, v_ref, s_ref):
    for i, head, cut in heads_of(per, width):
        down = column(cum_ref, head)
        tail = jnp.exp(down[-1:] - down)
        scaled = (k_ref[:, cut].astype(F32) * tail).astype(BF)
        s_ref[i] = dot_tn(scaled, v_ref[:, cut]).astype(BF)


def local_kernel(width, per, cum_ref, cumt_ref, q_ref, k_ref, v_ref, mix_ref):
    for i, head, cut in heads_of(per, width):
        down, across = column(cum_ref, head), cumt_ref[pl.ds(head, 1), :]
        for rows, seen in tiles(q_ref.shape[0], True):
            scores = dot_nt(q_ref[rows, cut], k_ref[seen, cut])
            weights = (scores * decay_tile(across, down, rows, seen, True)).astype(BF)
            mix_ref[rows, cut] = dot(weights, v_ref[seen, cut]).astype(mix_ref.dtype)


def norm_kernel(width, per, cum_ref, q_ref, g_ref, mix_ref, s_ref, att_ref, hg_ref, r_ref):
    for i, head, cut in heads_of(per, width):
        grow = jnp.exp(column(cum_ref, head))
        carried = grow * dot(q_ref[:, cut], s_ref[i])
        mixed = mix_ref[:, cut].astype(F32) + carried
        grad = g_ref[:, cut].astype(F32)
        scale = lax.rsqrt(jnp.mean(mixed * mixed, axis=-1, keepdims=True) + 1e-06)
        projection = jnp.mean(grad * mixed, axis=-1, keepdims=True)
        att_ref[:, cut] = (mixed * scale).astype(BF)
        head_grad = (scale * grad - mixed * (scale * scale * scale * projection)).astype(BF)
        hg_ref[:, cut] = head_grad
        grown = (q_ref[:, cut].astype(F32) * grow).astype(BF)
        r_ref[i] = dot_tn(grown, head_grad).astype(BF)


def back_query_kernel(width, per, cum_ref, cumt_ref, k_ref, v_ref, hg_ref, s_ref, qg_ref):
    for i, head, cut in heads_of(per, width):
        down, across = column(cum_ref, head), cumt_ref[pl.ds(head, 1), :]
        grow = jnp.exp(down)
        for rows, seen in tiles(k_ref.shape[0], True):
            pairs = dot_nt(hg_ref[rows, cut], v_ref[seen, cut])
            pairs = (pairs * decay_tile(across, down, rows, seen, True)).astype(BF)
            carried = grow[rows] * dot_nt(hg_ref[rows, cut], s_ref[i])
            qg_ref[rows, cut] = (dot(pairs, k_ref[seen, cut]) + carried).astype(BF)


def back_keys_kernel(width, per, cum_ref, cumt_ref, q_ref, k_ref, v_ref, hg_ref, kg_ref, vg_ref):
    for i, head, cut in heads_of(per, width):
        down, across = column(cum_ref, head), cumt_ref[pl.ds(head, 1), :]
        for rows, seen in tiles(q_ref.shape[0], False):
            decay = decay_tile(across, down, rows, seen, False)
            pairs = (dot_nt(v_ref[rows, cut], hg_ref[seen, cut]) * decay).astype(BF)
            kg_ref[rows, cut] = dot(pairs, q_ref[seen, cut]).astype(kg_ref.dtype)
            weights = (dot_nt(k_ref[rows, cut], q_ref[seen, cut]) * decay).astype(BF)
            vg_ref[rows, cut] = dot(weights, hg_ref[seen, cut]).astype(vg_ref.dtype)


def close_kernel(width, per, cum_ref, k_ref, v_ref, kl_ref, vl_ref, r_ref, kg_ref, vg_ref):
    for i, head, cut in heads_of(per, width):
        down = column(cum_ref, head)
        tail = jnp.exp(down[-1:] - down)
        key_carried = tail * dot_nt(v_ref[:, cut], r_ref[i])
        value_carried = tail * dot(k_ref[:, cut], r_ref[i])
        kg_ref[:, cut] = (kl_ref[:, cut].astype(F32) + key_carried).astype(BF)
        vg_ref[:, cut] = (vl_ref[:, cut].astype(F32) + value_carried).astype(BF)


def per_head(kernel, args, kinds, outs, tokens, heads, width, per, name, limit=60):
    specs = {
        "cum": pl.BlockSpec((tokens, heads), lambda j: (0, 0)),
        "cumt": pl.BlockSpec((heads, tokens), lambda j: (0, 0)),
        "col": pl.BlockSpec((tokens, width * per), lambda j: (0, j)),
        "state": pl.BlockSpec((per, width, width), lambda j: (j, 0, 0)),
    }
    shapes = {"col": (tokens, heads * width), "state": (heads, width, width)}
    return pl.pallas_call(
        functools.partial(kernel, width, per),
        grid=(heads // per,),
        in_specs=[specs[k] for k in kinds],
        out_specs=[specs[k] for k in outs],
        out_shape=[jax.ShapeDtypeStruct(shapes[k], BF) for k in outs],
        compiler_params=params(limit),
        cost_estimate=SMALL,
        name=name,
    )(*args)


def feature_kernel(count, index_ref, kg_ref, vg_ref, kw_ref, vw_ref, *refs):
    total = dot_nt(kg_ref[...], kw_ref[...]) + dot_nt(vg_ref[...], vw_ref[...])
    for r in refs[:count]:
        total += r[...].astype(F32)
    refs[count][0] = total.astype(BF)


def feature_terms(indices, key_grad, value_grad, key_weight, value_weight, adds, span):
    tokens, proj = key_grad.shape
    tile = min(512, span)
    steps = span // tile
    whole = pl.BlockSpec((tokens, proj), lambda i, j, d: (0, 0))
    weight = pl.BlockSpec((tile, proj), lambda i, j, d: (d[i] * steps + j, 0))
    number = indices.shape[0]
    return pl.pallas_call(
        functools.partial(feature_kernel, len(adds)),
        grid_spec=pltpu.PrefetchScalarGridSpec(
            num_scalar_prefetch=1,
            grid=(number, steps),
            in_specs=[whole, whole, weight, weight]
            + [pl.BlockSpec((tokens, tile), lambda i, j, d: (0, j))] * len(adds),
            out_specs=pl.BlockSpec((1, tokens, tile), lambda i, j, d: (i, 0, j)),
        ),
        out_shape=jax.ShapeDtypeStruct((number, tokens, span), BF),
        compiler_params=params(60),
        cost_estimate=SMALL,
        name="feature_terms",
    )(indices, key_grad, value_grad, key_weight, value_weight, *adds)


def weight_kernel(index_ref, fo_ref, fp_ref, go_ref, gp_ref, out_ref):
    total = dot(fo_ref[0], go_ref[...]) + dot(fp_ref[0], gp_ref[...])
    out_ref[0] = total.astype(out_ref.dtype)


def weight_terms(slots, own_t, partner_t, grad, partner_grad, kind):
    tokens, proj = grad.shape
    span = own_t.shape[1]
    number = slots.shape[0]
    tile = min(512, proj)
    rows = pl.BlockSpec((1, span, tokens), lambda j, i, d: (d[i], 0, 0))
    cols = pl.BlockSpec((tokens, tile), lambda j, i, d: (0, j))
    return pl.pallas_call(
        weight_kernel,
        grid_spec=pltpu.PrefetchScalarGridSpec(
            num_scalar_prefetch=1,
            grid=(proj // tile, number),
            in_specs=[rows, rows, cols, cols],
            out_specs=pl.BlockSpec((1, span, tile), lambda j, i, d: (i, 0, j)),
        ),
        out_shape=jax.ShapeDtypeStruct((number, span, proj), kind),
        compiler_params=params(60),
        cost_estimate=SMALL,
        name="weight_terms",
    )(slots, own_t, partner_t, grad, partner_grad)


def turn_kernel(aliased, core_ref, *refs):
    shards, (own_ref, other_ref, held, turned, sem) = refs[aliased:-5], refs[-5:]
    core = core_ref[0]
    for i, shard in enumerate(shards):

        @pl.when(pl.program_id(0) == i)
        def _():
            copy = pltpu.make_async_copy(shard, held, sem)
            copy.start()
            copy.wait()

    turned[...] = held[...].T
    rows = own_ref.shape[1]
    own_ref[0] = turned[pl.ds(pl.multiple_of(core * rows, rows), rows), :]
    other_ref[0] = turned[pl.ds(pl.multiple_of((1 - core) * rows, rows), rows), :]


def turn_features(core, shards, first, slots, held=()):
    tokens, depth = shards[0].shape
    half = pl.BlockSpec((1, depth // 2, tokens), lambda j, d: (first + j, 0, 0))
    aliased = len(held)
    return pl.pallas_call(
        functools.partial(turn_kernel, aliased),
        grid_spec=pltpu.PrefetchScalarGridSpec(
            num_scalar_prefetch=1,
            grid=(len(shards),),
            in_specs=[pl.BlockSpec(memory_space=pl.ANY)] * (aliased + len(shards)),
            out_specs=[half, half],
            scratch_shapes=[
                pltpu.VMEM((tokens, depth), BF),
                pltpu.VMEM((depth, tokens), BF),
                pltpu.SemaphoreType.DMA,
            ],
        ),
        out_shape=[jax.ShapeDtypeStruct((slots, depth // 2, tokens), BF)] * 2,
        input_output_aliases={1 + i: i for i in range(aliased)},
        compiler_params=params(60),
        cost_estimate=SMALL,
        name="turn_features",
    )(core[None], *held, *shards)


def merge_states(earlier, later):
    return (earlier[0] * later[0], later[0][:, None, None] * earlier[1] + later[1])


def entering(x, axis, backward):
    count = lax.axis_size(axis)
    place = lax.axis_index(axis)
    ahead = count - 1 - place if backward else place
    gathered = tuple(lax.all_gather(a.astype(BF), axis) for a in x)
    state = (jnp.ones_like(x[0]), jnp.zeros_like(x[1]))

    def one(hop, state):
        source = count - 1 - hop if backward else hop
        item = tuple(
            lax.dynamic_index_in_dim(a, source, 0, False).astype(own.dtype)
            for a, own in zip(gathered, x)
        )
        return merge_states(state, item)

    return lax.fori_loop(0, ahead, one, state)[1].astype(BF)


def swap(x, bit, keep=None):
    pairs = [(s, s ^ bit) for s in range(8) if keep is None or keep(s)]
    return lax.ppermute(x, "seq", pairs)


def gather_totals(own):
    place = lax.axis_index("seq")
    held = own[None]
    for bit in (1, 2, 4):
        other = swap(held, bit)
        upper = (place & bit) != 0
        held = jnp.concatenate(
            [jnp.where(upper, other, held), jnp.where(upper, held, other)], axis=0
        )
    return held


def entering_chips(state, totals, backward, first_wait, second_wait):
    place = lax.axis_index("seq")
    core = lax.rem(place, 2)
    half = state.shape[0] // 2
    ahead_of = (lambda bit: (place & bit) == 0) if backward else (lambda bit: (place & bit) != 0)
    decay = jnp.exp(totals)[:, :, None, None]

    def halves(a):
        return lax.dynamic_slice_in_dim(a, core * half, half, 0)

    def join(own, other, bit, own_factor, other_factor):
        late = ahead_of(bit)
        own, other = own.astype(F32), other.astype(F32)
        return jnp.where(late, own_factor * other + own, other_factor * own + other)

    partner = swap(state, 1)
    own_decay, partner_decay = decay[place], decay[place ^ 1]
    chip = join(halves(state), halves(partner), 1, halves(own_decay), halves(partner_decay)).astype(BF)
    beside, first_wait = together(swap(chip, 2), first_wait)
    chip_decay = halves(own_decay * partner_decay)
    beside_decay = halves(decay[place ^ 2] * decay[place ^ 3])
    pair = join(chip, beside, 2, chip_decay, beside_decay).astype(BF)
    keep = (lambda s: (s & 4) != 0) if backward else (lambda s: (s & 4) == 0)
    passed, second_wait = together(swap(pair, 4, keep), second_wait)
    passed = passed.astype(F32)
    entered = jnp.where(ahead_of(2), beside_decay * passed + beside.astype(F32), passed).astype(BF)
    other = swap(entered, 1)
    whole = jnp.where(
        core == 0, jnp.concatenate([entered, other]), jnp.concatenate([other, entered])
    )
    step = partner_decay * whole.astype(F32) + partner.astype(F32)
    return jnp.where(ahead_of(1), step.astype(BF), whole), first_wait, second_wait


def line_pairs(count, step, up):
    if up:
        return [(i, i + 1) for i in range(step - 1, count - 1)]
    return [(i, i - 1) for i in range(1, count - step + 1)]


def scatter_pairs(count, step, up):
    if up:
        return [(i, i + 1) for i in range(0, min(step, count - 1))]
    return [(i, i - 1) for i in range(max(1, count - step), count)]


def per_device(features, key_weight, value_weight, queries, log_decay, out_grad):
    tokens, proj = queries.shape
    depth = features.shape[1]
    model = key_weight.shape[0]
    heads = log_decay.shape[1]
    width = proj // heads
    per = 2 if heads % 2 == 0 else 1
    count = lax.axis_size("head")
    blocks = lax.axis_size("seq")
    here = lax.axis_index("head")
    place = lax.axis_index("seq")
    chips = blocks == 8 and model == 8 * 512 and count == 4

    cum = jnp.cumsum(log_decay, axis=0)
    cum_t = cum.T
    total = cum[-1]

    up = down = features

    def rows_of(weight, index):
        return lax.dynamic_slice_in_dim(weight, index * depth, depth, 0)

    def project(sums, shard, index):
        key_part = dot(shard, rows_of(key_weight, index))
        value_part = dot(shard, rows_of(value_weight, index))
        return [key_part, value_part] if sums is None else [sums[0] + key_part, sums[1] + value_part]

    if chips:
        core = lax.rem(place, 2)
        totals = gather_totals(total)
        chip = place // 2

        def slots_of(*targets):
            offsets = jnp.stack(targets) - here
            far = jnp.abs(offsets)
            return jnp.where(far < 2, jnp.where(offsets < 0, 2, far), far + 1)

        ranks = (
            slots_of(chip ^ 3, chip ^ 1),
            slots_of(chip ^ 3, chip ^ 2),
            slots_of(chip ^ 1),
            slots_of(chip ^ 2),
            slots_of(chip),
        )
    sums = project(None, features, here)
    slots = [features]
    turned = ()
    merged = None
    for step in range(1, count):
        upward, downward = line_pairs(count, step, True), line_pairs(count, step, False)
        if merged is None:
            up = lax.ppermute(up, "head", upward)
            down = lax.ppermute(down, "head", downward)
            got = [up, down]
        else:
            got = [lax.ppermute(merged, "head", upward + downward)]
        if chips and step == count - 2:
            turned = turn_features(core, slots, 0, 5)
            got, sums, turned, totals, ranks = together(got, sums, turned, totals, ranks)
        else:
            got, sums = together(got, sums)
        if 2 * step >= count:
            index = jnp.where(here >= step, here - step, jnp.minimum(here + step, count - 1))
            merged = got[0] if len(got) == 1 else got[0] + got[1]
            shards = [(merged, index)]
        else:
            up, down = got
            shards = [
                (down, jnp.minimum(here + step, count - 1)),
                (up, jnp.maximum(here - step, 0)),
            ]
        slots += [shard for shard, _ in shards]
        for shard, index in shards:
            sums = project(sums, shard, index)
    key_sum, value_sum = sums
    keys, values = key_sum.astype(BF), value_sum.astype(BF)

    each = functools.partial(per_head, tokens=tokens, heads=heads, width=width, per=per)
    (local_state,) = each(
        state_kernel,
        (cum, keys, values),
        ("cum", "col", "col"),
        ("state",),
        name="local_state",
        limit=16,
    )
    (mix,) = each(
        local_kernel,
        (cum, cum_t, queries, keys, values),
        ("cum", "cumt", "col", "col", "col"),
        ("col",),
        name="local_mix",
    )
    if chips:
        own_t, other_t = turn_features(core, slots[3:], 3, 5, turned)
        incoming, mix, (own_t, other_t) = entering_chips(
            local_state, totals, False, mix, (own_t, other_t)
        )
        incoming, other_t = together(incoming, other_t)
        partner_t = swap(other_t, 1)
    else:
        incoming = entering((jnp.exp(total), local_state.astype(F32)), "seq", False)
    attended, head_grad, local_reverse = each(
        norm_kernel,
        (cum, queries, out_grad, mix, incoming),
        ("cum", "col", "col", "col", "state"),
        ("col", "col", "state"),
        name="norm_grad",
    )
    (query_grad,) = each(
        back_query_kernel,
        (cum, cum_t, keys, values, head_grad, incoming),
        ("cum", "cumt", "col", "col", "col", "state"),
        ("col",),
        name="back_query",
    )
    key_local, value_local = each(
        back_keys_kernel,
        (cum, cum_t, queries, keys, values, head_grad),
        ("cum", "cumt", "col", "col", "col", "col"),
        ("col", "col"),
        name="back_keys",
    )
    if chips:
        outgoing, query_grad, (key_local, value_local, partner_t) = entering_chips(
            local_reverse, totals, True, query_grad, (key_local, value_local, partner_t)
        )
    else:
        outgoing = entering((jnp.exp(total), local_reverse.astype(F32)), "seq", True)
    key_grad, value_grad = each(
        close_kernel,
        (cum, keys, values, key_local, value_local, outgoing),
        ("cum", "col", "col", "col", "col", "state"),
        ("col", "col"),
        name="close_back",
    )

    def terms(*indices):
        return feature_terms(
            jnp.stack(indices), key_grad, value_grad, key_weight, value_weight, (), depth
        )

    def add(*terms):
        return sum(t.astype(F32) for t in terms).astype(BF)

    def scatter_indices(step):
        upward = jnp.minimum(here + count - step, count - 1)
        downward = jnp.maximum(here - count + step, 0)
        return upward, downward

    def either_term(step):
        upward, downward = scatter_indices(step)
        return terms(jnp.where(here < step, upward, downward))[0]

    def send(step, up_sum, down_sum):
        upward, downward = scatter_pairs(count, step, True), scatter_pairs(count, step, False)
        if 2 * step < count - 1:
            return (lax.ppermute(up_sum, "head", upward + downward),)
        return lax.ppermute(up_sum, "head", upward), lax.ppermute(down_sum, "head", downward)

    norm = (tokens * blocks) ** (-0.5)
    if not chips:
        got = ()
        for step in range(1, count):
            if 2 * step <= count:
                total = add(either_term(step), *got)
                got = send(step, total, total)
            else:
                up_term, down_term = terms(*scatter_indices(step))
                got = send(step, add(up_term, got[0]), add(down_term, got[1]))
        feature_grad = add(terms(here)[0], *got)
        gathered = lax.all_gather(features, "head", axis=1, tiled=True)
        both = jnp.concatenate([key_grad, value_grad], axis=1)
        summed = lax.psum_scatter(
            lax.dot_general(gathered, both, TN, preferred_element_type=F32).astype(BF),
            "seq",
            scatter_dimension=0,
            tiled=True,
        ).astype(F32)
        summed = summed * norm
        return attended, query_grad, feature_grad, summed[:, :proj], summed[:, proj:]

    away_x, away_y, one_x, one_y, home = ranks
    partner_key, partner_value = swap(key_grad, 1), swap(value_grad, 1)

    def blocks_for(slot, grad, partner_grad, kind=BF):
        return weight_terms(slot, own_t, partner_t, grad, partner_grad, kind)

    first = either_term(1)
    got = send(1, first, first)
    key_away = blocks_for(away_x, key_grad, partner_key)
    key_away, value_grad, partner_value = together(key_away, value_grad, partner_value)
    got_key = swap(key_away, 2)
    value_away = blocks_for(away_y, value_grad, partner_value)
    value_away, key_grad = together(value_away, key_grad)
    got_value = swap(value_away, 4)
    second = either_term(2)
    got, second = together(got, second)
    total = add(second, *got)
    total, value_grad = together(total, value_grad)
    got = send(2, total, total)
    ahead = terms(*scatter_indices(3))
    ahead, key_grad, value_grad = together(ahead, key_grad, value_grad)
    key_pass = blocks_for(one_y, key_grad, partner_key)
    value_pass = blocks_for(one_x, value_grad, partner_value)
    got, key_pass, value_pass = together(got, key_pass, value_pass)
    up_sum, down_sum = add(ahead[0], got[0]), add(ahead[1], got[1])
    up_sum, down_sum, got_key = together(up_sum, down_sum, got_key)
    up, down = send(3, up_sum, down_sum)
    key_sent = add(key_pass[0], got_key[0])
    key_sent, got_value = together(key_sent, got_value)
    got_key_pass = swap(key_sent, 4)
    value_sent = add(value_pass[0], got_value[0])
    value_sent, key_grad, value_grad = together(value_sent, key_grad, value_grad)
    got_value_pass = swap(value_sent, 2)
    key_own = blocks_for(home, key_grad, partner_key, F32)[0]
    value_own = blocks_for(home, value_grad, partner_value, F32)[0]
    feature_own = terms(here)[0]
    up, key_own, value_own = together(up, key_own, value_own)
    feature_grad = add(feature_own, up, down)
    got_key_pass, feature_grad = together(got_key_pass, feature_grad)
    key_out = (key_own + got_key[1].astype(F32) + got_key_pass.astype(F32)) * norm
    got_value_pass, key_out = together(got_value_pass, key_out)
    value_out = (value_own + got_value[1].astype(F32) + got_value_pass.astype(F32)) * norm
    return attended, query_grad, feature_grad, key_out, value_out


def solution(mesh):
    spread = P("seq", "head")
    return jax.shard_map(
        per_device,
        mesh=mesh,
        in_specs=(spread, P(None, "head"), P(None, "head"), spread, spread, spread),
        out_specs=(spread,) * 5,
        check_vma=False,
    )
```

```python
import functools

import jax
import jax.numpy as jnp
from jax import lax
from jax.experimental import pallas as pl
from jax.experimental.pallas import tpu as pltpu
from jax.sharding import PartitionSpec as P

BF = jnp.bfloat16
F32 = jnp.float32
NT = (((1,), (1,)), ((), ()))
TN = (((0,), (0,)), ((), ()))
MIB = 1024 * 1024


def dot(a, b):
    return jnp.dot(a, b, preferred_element_type=F32)


def dot_nt(a, b):
    return lax.dot_general(a, b, NT, preferred_element_type=F32)


def dot_tn(a, b):
    return lax.dot_general(a, b, TN, preferred_element_type=F32)


def params(limit=16):
    return pltpu.CompilerParams(vmem_limit_bytes=limit * MIB)


def together(*arrays):
    return lax.optimization_barrier(arrays)


SMALL = pl.CostEstimate(flops=1, bytes_accessed=1, transcendentals=0)


def tiles(tokens, causal):
    tile = min(256, tokens)
    for row in range(tokens // tile):
        first, last = row * tile, (row + 1) * tile
        yield slice(first, last), slice(0, last) if causal else slice(first, tokens)


def column(cum_ref, head):
    lanes = lax.broadcasted_iota(jnp.int32, cum_ref.shape, 1)
    return jnp.sum(jnp.where(lanes == head, cum_ref[...], 0.0), axis=1, keepdims=True)


def decay_tile(across, down, rows, seen, causal):
    shape = (rows.stop - rows.start, seen.stop - seen.start)
    one = rows.start + lax.broadcasted_iota(jnp.int32, shape, 0)
    two = seen.start + lax.broadcasted_iota(jnp.int32, shape, 1)
    gap = down[rows] - across[:, seen]
    if causal:
        return jnp.where(two <= one, jnp.exp(gap), 0.0)
    return jnp.where(one <= two, jnp.exp(-gap), 0.0)


def each_head(per, width, body, group=2):
    group = group if per % group == 0 else 1

    def some(number, carry):
        for j in range(group):
            i = number * group + j
            cut = pl.ds(pl.multiple_of(i * width, width), width)
            body(i, pl.program_id(0) * per + i, cut)
        return carry

    lax.fori_loop(0, per // group, some, 0)


def state_kernel(width, per, cum_ref, k_ref, v_ref, s_ref):
    def one(i, head, cut):
        down = column(cum_ref, head)
        tail = jnp.exp(down[-1:] - down)
        scaled = (k_ref[:, cut].astype(F32) * tail).astype(BF)
        s_ref[i] = dot_tn(scaled, v_ref[:, cut]).astype(BF)

    each_head(per, width, one)


def local_kernel(width, per, cum_ref, cumt_ref, q_ref, k_ref, v_ref, mix_ref):
    def one(i, head, cut):
        down, across = column(cum_ref, head), cumt_ref[pl.ds(head, 1), :]
        for rows, seen in tiles(q_ref.shape[0], True):
            scores = dot_nt(q_ref[rows, cut], k_ref[seen, cut])
            weights = (scores * decay_tile(across, down, rows, seen, True)).astype(BF)
            mix_ref[rows, cut] = dot(weights, v_ref[seen, cut]).astype(mix_ref.dtype)

    each_head(per, width, one, 4)


def norm_kernel(width, per, cum_ref, q_ref, g_ref, mix_ref, s_ref, att_ref, hg_ref, r_ref):
    def one(i, head, cut):
        grow = jnp.exp(column(cum_ref, head))
        carried = grow * dot(q_ref[:, cut], s_ref[i])
        mixed = mix_ref[:, cut].astype(F32) + carried
        grad = g_ref[:, cut].astype(F32)
        scale = lax.rsqrt(jnp.mean(mixed * mixed, axis=-1, keepdims=True) + 1e-06)
        projection = jnp.mean(grad * mixed, axis=-1, keepdims=True)
        att_ref[:, cut] = (mixed * scale).astype(BF)
        head_grad = (scale * grad - mixed * (scale * scale * scale * projection)).astype(BF)
        hg_ref[:, cut] = head_grad
        grown = (q_ref[:, cut].astype(F32) * grow).astype(BF)
        r_ref[i] = dot_tn(grown, head_grad).astype(BF)

    each_head(per, width, one, 4)


def back_query_kernel(width, per, cum_ref, cumt_ref, k_ref, v_ref, hg_ref, s_ref, qg_ref):
    def one(i, head, cut):
        down, across = column(cum_ref, head), cumt_ref[pl.ds(head, 1), :]
        grow = jnp.exp(down)
        for rows, seen in tiles(k_ref.shape[0], True):
            pairs = dot_nt(hg_ref[rows, cut], v_ref[seen, cut])
            pairs = (pairs * decay_tile(across, down, rows, seen, True)).astype(BF)
            carried = grow[rows] * dot_nt(hg_ref[rows, cut], s_ref[i])
            qg_ref[rows, cut] = (dot(pairs, k_ref[seen, cut]) + carried).astype(BF)

    each_head(per, width, one, 4)


def back_keys_kernel(width, per, cum_ref, cumt_ref, q_ref, k_ref, v_ref, hg_ref, kg_ref, vg_ref):
    def one(i, head, cut):
        down, across = column(cum_ref, head), cumt_ref[pl.ds(head, 1), :]
        for rows, seen in tiles(q_ref.shape[0], False):
            decay = decay_tile(across, down, rows, seen, False)
            pairs = (dot_nt(v_ref[rows, cut], hg_ref[seen, cut]) * decay).astype(BF)
            kg_ref[rows, cut] = dot(pairs, q_ref[seen, cut]).astype(kg_ref.dtype)
            weights = (dot_nt(k_ref[rows, cut], q_ref[seen, cut]) * decay).astype(BF)
            vg_ref[rows, cut] = dot(weights, hg_ref[seen, cut]).astype(vg_ref.dtype)

    each_head(per, width, one)


def close_kernel(width, per, cum_ref, k_ref, v_ref, kl_ref, vl_ref, r_ref, kg_ref, vg_ref):
    def one(i, head, cut):
        down = column(cum_ref, head)
        tail = jnp.exp(down[-1:] - down)
        key_carried = tail * dot_nt(v_ref[:, cut], r_ref[i])
        value_carried = tail * dot(k_ref[:, cut], r_ref[i])
        kg_ref[:, cut] = (kl_ref[:, cut].astype(F32) + key_carried).astype(BF)
        vg_ref[:, cut] = (vl_ref[:, cut].astype(F32) + value_carried).astype(BF)

    each_head(per, width, one)


def per_head(kernel, args, kinds, outs, tokens, heads, width, per, name, limit=60):
    specs = {
        "cum": pl.BlockSpec((tokens, heads), lambda j: (0, 0)),
        "cumt": pl.BlockSpec((heads, tokens), lambda j: (0, 0)),
        "col": pl.BlockSpec((tokens, width * per), lambda j: (0, j)),
        "state": pl.BlockSpec((per, width, width), lambda j: (j, 0, 0)),
    }
    shapes = {"col": (tokens, heads * width), "state": (heads, width, width)}
    return pl.pallas_call(
        functools.partial(kernel, width, per),
        grid=(heads // per,),
        in_specs=[specs[k] for k in kinds],
        out_specs=[specs[k] for k in outs],
        out_shape=[jax.ShapeDtypeStruct(shapes[k], BF) for k in outs],
        compiler_params=params(limit),
        cost_estimate=SMALL,
        name=name,
    )(*args)


def feature_kernel(index_ref, kg_ref, vg_ref, kw_ref, vw_ref, out_ref):
    grads = jnp.concatenate([kg_ref[...], vg_ref[...]], axis=1)
    weights = jnp.concatenate([kw_ref[...], vw_ref[...]], axis=1)
    out_ref[0] = dot_nt(grads, weights).astype(BF)


def feature_terms(indices, key_grad, value_grad, key_weight, value_weight, span):
    tokens, proj = key_grad.shape
    tile = min(512, span)
    steps = span // tile
    number = indices.shape[0]
    whole = pl.BlockSpec((tokens, proj), lambda i, j, d: (0, 0))
    weight = pl.BlockSpec((tile, proj), lambda i, j, d: (d[i] * steps + j, 0))
    return pl.pallas_call(
        feature_kernel,
        grid_spec=pltpu.PrefetchScalarGridSpec(
            num_scalar_prefetch=1,
            grid=(number, steps),
            in_specs=[whole, whole, weight, weight],
            out_specs=pl.BlockSpec((1, tokens, tile), lambda i, j, d: (i, 0, j)),
        ),
        out_shape=jax.ShapeDtypeStruct((number, tokens, span), BF),
        compiler_params=params(60),
        cost_estimate=SMALL,
        name="feature_terms",
    )(indices, key_grad, value_grad, key_weight, value_weight)


def weight_kernel(count, index_ref, fo_ref, fp_ref, go_ref, gp_ref, *refs):
    turned = jnp.concatenate([fo_ref[0], fp_ref[0]], axis=1)
    total = dot(turned, jnp.concatenate([go_ref[...], gp_ref[...]], axis=0))
    for r in refs[:count]:
        total += r[0].astype(F32)
    refs[count][0] = total.astype(BF)


def weight_terms(slots, own_t, partner_t, grad, partner_grad, adds=()):
    tokens, proj = grad.shape
    span = own_t.shape[1]
    number = slots.shape[0]
    tile = proj
    rows = pl.BlockSpec((1, span, tokens), lambda j, i, d: (d[i], 0, 0))
    cols = pl.BlockSpec((tokens, tile), lambda j, i, d: (0, j))
    extra = [
        pl.BlockSpec((1, span, tile), lambda j, i, d, last=a.shape[0] - 1: (last, 0, j)) for a in adds
    ]
    return pl.pallas_call(
        functools.partial(weight_kernel, len(adds)),
        grid_spec=pltpu.PrefetchScalarGridSpec(
            num_scalar_prefetch=1,
            grid=(proj // tile, number),
            in_specs=[rows, rows, cols, cols] + extra,
            out_specs=pl.BlockSpec((1, span, tile), lambda j, i, d: (i, 0, j)),
        ),
        out_shape=jax.ShapeDtypeStruct((number, span, proj), BF),
        compiler_params=params(60),
        cost_estimate=SMALL,
        name="weight_terms",
    )(slots, own_t, partner_t, grad, partner_grad, *adds)


def turn_kernel(aliased, core_ref, *refs):
    shards, (own_ref, other_ref, held, turned, sem) = refs[aliased:-5], refs[-5:]
    core = core_ref[0]
    for i, shard in enumerate(shards):

        @pl.when(pl.program_id(0) == i)
        def _():
            copy = pltpu.make_async_copy(shard, held, sem)
            copy.start()
            copy.wait()

    turned[...] = held[...].T
    rows = own_ref.shape[1]
    own_ref[0] = turned[pl.ds(pl.multiple_of(core * rows, rows), rows), :]
    other_ref[0] = turned[pl.ds(pl.multiple_of((1 - core) * rows, rows), rows), :]


def turn_features(core, shards, first, slots, held=()):
    tokens, depth = shards[0].shape
    half = pl.BlockSpec((1, depth // 2, tokens), lambda j, d: (first + j, 0, 0))
    aliased = len(held)
    return pl.pallas_call(
        functools.partial(turn_kernel, aliased),
        grid_spec=pltpu.PrefetchScalarGridSpec(
            num_scalar_prefetch=1,
            grid=(len(shards),),
            in_specs=[pl.BlockSpec(memory_space=pl.ANY)] * (aliased + len(shards)),
            out_specs=[half, half],
            scratch_shapes=[
                pltpu.VMEM((tokens, depth), BF),
                pltpu.VMEM((depth, tokens), BF),
                pltpu.SemaphoreType.DMA,
            ],
        ),
        out_shape=[jax.ShapeDtypeStruct((slots, depth // 2, tokens), BF)] * 2,
        input_output_aliases={1 + i: i for i in range(aliased)},
        compiler_params=params(60),
        cost_estimate=SMALL,
        name="turn_features",
    )(core[None], *held, *shards)


def merge_states(earlier, later):
    return (earlier[0] * later[0], later[0][:, None, None] * earlier[1] + later[1])


def entering(x, axis, backward):
    count = lax.axis_size(axis)
    place = lax.axis_index(axis)
    ahead = count - 1 - place if backward else place
    gathered = tuple(lax.all_gather(a.astype(BF), axis) for a in x)
    state = (jnp.ones_like(x[0]), jnp.zeros_like(x[1]))

    def one(hop, state):
        source = count - 1 - hop if backward else hop
        item = tuple(
            lax.dynamic_index_in_dim(a, source, 0, False).astype(own.dtype)
            for a, own in zip(gathered, x)
        )
        return merge_states(state, item)

    return lax.fori_loop(0, ahead, one, state)[1].astype(BF)


def swap(x, bit, keep=None):
    pairs = [(s, s ^ bit) for s in range(8) if keep is None or keep(s)]
    return lax.ppermute(x, "seq", pairs)


def gather_totals(own):
    place = lax.axis_index("seq")
    held = own[None]
    for bit in (1, 2, 4):
        other = swap(held, bit)
        upper = (place & bit) != 0
        held = jnp.concatenate(
            [jnp.where(upper, other, held), jnp.where(upper, held, other)], axis=0
        )
    return held


def entering_chips(state, totals, backward, first_wait, second_wait):
    place = lax.axis_index("seq")
    core = lax.rem(place, 2)
    half = state.shape[0] // 2
    ahead_of = (lambda bit: (place & bit) == 0) if backward else (lambda bit: (place & bit) != 0)
    decay = jnp.exp(totals)[:, :, None, None]

    def halves(a):
        return lax.dynamic_slice_in_dim(a, core * half, half, 0)

    def join(own, other, bit, own_factor, other_factor):
        late = ahead_of(bit)
        own, other = own.astype(F32), other.astype(F32)
        return jnp.where(late, own_factor * other + own, other_factor * own + other)

    partner = swap(state, 1)
    own_decay, partner_decay = decay[place], decay[place ^ 1]
    chip = join(halves(state), halves(partner), 1, halves(own_decay), halves(partner_decay)).astype(BF)
    beside, first_wait = together(swap(chip, 2), first_wait)
    chip_decay = halves(own_decay * partner_decay)
    beside_decay = halves(decay[place ^ 2] * decay[place ^ 3])
    pair = join(chip, beside, 2, chip_decay, beside_decay).astype(BF)
    keep = (lambda s: (s & 4) != 0) if backward else (lambda s: (s & 4) == 0)
    passed, second_wait = together(swap(pair, 4, keep), second_wait)
    passed = passed.astype(F32)
    entered = jnp.where(ahead_of(2), beside_decay * passed + beside.astype(F32), passed).astype(BF)
    other = swap(entered, 1)
    whole = jnp.where(
        core == 0, jnp.concatenate([entered, other]), jnp.concatenate([other, entered])
    )
    step = partner_decay * whole.astype(F32) + partner.astype(F32)
    return jnp.where(ahead_of(1), step.astype(BF), whole), first_wait, second_wait


def line_pairs(count, step, up):
    if up:
        return [(i, i + 1) for i in range(step - 1, count - 1)]
    return [(i, i - 1) for i in range(1, count - step + 1)]


def scatter_pairs(count, step, up):
    if up:
        return [(i, i + 1) for i in range(0, min(step, count - 1))]
    return [(i, i - 1) for i in range(max(1, count - step), count)]


def per_device(features, key_weight, value_weight, queries, log_decay, out_grad):
    tokens, proj = queries.shape
    depth = features.shape[1]
    model = key_weight.shape[0]
    heads = log_decay.shape[1]
    width = proj // heads
    per = 4 if heads % 4 == 0 else 1
    count = lax.axis_size("head")
    blocks = lax.axis_size("seq")
    here = lax.axis_index("head")
    place = lax.axis_index("seq")
    chips = blocks == 8 and model == 8 * 512 and count == 4

    cum = jnp.cumsum(log_decay, axis=0)
    cum_t = cum.T
    total = cum[-1]

    up = down = features

    def rows_of(weight, index):
        return lax.dynamic_slice_in_dim(weight, index * depth, depth, 0)

    def project(sums, shard, key_rows, value_rows):
        parts = [dot(shard, key_rows), dot(shard, value_rows)]
        return parts if sums is None else [a + b for a, b in zip(sums, parts)]

    def both_rows(index):
        return rows_of(key_weight, index), rows_of(value_weight, index)

    if chips:
        core = lax.rem(place, 2)
        totals = gather_totals(total)
        chip = place // 2

        def slots_of(*targets):
            offsets = jnp.stack(targets) - here
            far = jnp.abs(offsets)
            return jnp.where(far < 2, jnp.where(offsets < 0, 2, far), far + 1)

        ranks = (
            slots_of(chip ^ 3, chip ^ 1),
            slots_of(chip ^ 3, chip ^ 2),
            slots_of(chip ^ 1),
            slots_of(chip ^ 2),
            slots_of(chip),
        )
    sums = project(None, features, *both_rows(here))
    slots = [features]
    turned = ()
    merged = None
    for step in range(1, count):
        upward, downward = line_pairs(count, step, True), line_pairs(count, step, False)
        if merged is None:
            up = lax.ppermute(up, "head", upward)
            down = lax.ppermute(down, "head", downward)
            got = [up, down]
        else:
            got = [lax.ppermute(merged, "head", upward + downward)]
        if 2 * step >= count:
            index = jnp.where(here >= step, here - step, jnp.minimum(here + step, count - 1))
            rows = [both_rows(index)]
        else:
            rows = [
                both_rows(jnp.minimum(here + step, count - 1)),
                both_rows(jnp.maximum(here - step, 0)),
            ]
        if chips and step == count - 2:
            turned = turn_features(core, slots, 0, 5)
            got, sums, turned, totals, ranks, cum, cum_t = together(
                got, sums, turned, totals, ranks, cum, cum_t
            )
        elif step == count - 1:
            got, sums, rows = together(got, sums, rows)
        else:
            got, sums = together(got, sums)
        if 2 * step >= count:
            merged = got[0] if len(got) == 1 else got[0] + got[1]
            shards = [merged]
        else:
            up, down = got
            shards = [down, up]
        slots += shards
        for shard, pair in zip(shards, rows):
            sums = project(sums, shard, *pair)
    key_sum, value_sum = sums
    keys, values = key_sum.astype(BF), value_sum.astype(BF)

    each = functools.partial(per_head, tokens=tokens, heads=heads, width=width, per=per)
    (local_state,) = each(
        state_kernel,
        (cum, keys, values),
        ("cum", "col", "col"),
        ("state",),
        name="local_state",
        limit=16,
    )
    (mix,) = each(
        local_kernel,
        (cum, cum_t, queries, keys, values),
        ("cum", "cumt", "col", "col", "col"),
        ("col",),
        name="local_mix",
    )
    if chips:
        own_t, other_t = turn_features(core, slots[3:], 3, 5, turned)
        incoming, mix, (own_t, other_t) = entering_chips(
            local_state, totals, False, mix, (own_t, other_t)
        )
        incoming, other_t = together(incoming, other_t)
        partner_t = swap(other_t, 1)
    else:
        incoming = entering((jnp.exp(total), local_state.astype(F32)), "seq", False)
    attended, head_grad, local_reverse = each(
        norm_kernel,
        (cum, queries, out_grad, mix, incoming),
        ("cum", "col", "col", "col", "state"),
        ("col", "col", "state"),
        name="norm_grad",
    )
    (query_grad,) = each(
        back_query_kernel,
        (cum, cum_t, keys, values, head_grad, incoming),
        ("cum", "cumt", "col", "col", "col", "state"),
        ("col",),
        name="back_query",
    )
    key_local, value_local = each(
        back_keys_kernel,
        (cum, cum_t, queries, keys, values, head_grad),
        ("cum", "cumt", "col", "col", "col", "col"),
        ("col", "col"),
        name="back_keys",
    )
    if chips:
        outgoing, query_grad, (key_local, value_local, partner_t) = entering_chips(
            local_reverse, totals, True, query_grad, (key_local, value_local, partner_t)
        )
    else:
        outgoing = entering((jnp.exp(total), local_reverse.astype(F32)), "seq", True)
    key_grad, value_grad = each(
        close_kernel,
        (cum, keys, values, key_local, value_local, outgoing),
        ("cum", "col", "col", "col", "col", "state"),
        ("col", "col"),
        name="close_back",
    )

    def terms(*indices):
        return feature_terms(
            jnp.stack(indices), key_grad, value_grad, key_weight, value_weight, depth
        )

    def add(*terms):
        return sum(t.astype(F32) for t in terms).astype(BF)

    def scatter_indices(step):
        upward = jnp.minimum(here + count - step, count - 1)
        downward = jnp.maximum(here - count + step, 0)
        return upward, downward

    def either_term(step):
        upward, downward = scatter_indices(step)
        return terms(jnp.where(here < step, upward, downward))[0]

    def send(step, up_sum, down_sum):
        upward, downward = scatter_pairs(count, step, True), scatter_pairs(count, step, False)
        if 2 * step < count - 1:
            return (lax.ppermute(up_sum, "head", upward + downward),)
        return lax.ppermute(up_sum, "head", upward), lax.ppermute(down_sum, "head", downward)

    norm = (tokens * blocks) ** (-0.5)
    if not chips:
        got = ()
        for step in range(1, count):
            if 2 * step <= count:
                total = add(either_term(step), *got)
                got = send(step, total, total)
            else:
                up_term, down_term = terms(*scatter_indices(step))
                got = send(step, add(up_term, got[0]), add(down_term, got[1]))
        feature_grad = add(terms(here)[0], *got)
        gathered = lax.all_gather(features, "head", axis=1, tiled=True)
        both = jnp.concatenate([key_grad, value_grad], axis=1)
        summed = lax.psum_scatter(
            lax.dot_general(gathered, both, TN, preferred_element_type=F32).astype(BF),
            "seq",
            scatter_dimension=0,
            tiled=True,
        ).astype(F32)
        summed = summed * norm
        return attended, query_grad, feature_grad, summed[:, :proj], summed[:, proj:]

    away_x, away_y, one_x, one_y, home = ranks
    partner_key, partner_value = swap(key_grad, 1), swap(value_grad, 1)

    def blocks_for(slot, grad, partner_grad, adds=()):
        return weight_terms(slot, own_t, partner_t, grad, partner_grad, adds)

    first = either_term(1)
    got = send(1, first, first)
    key_away = blocks_for(away_x, key_grad, partner_key)
    key_away, value_grad, partner_value = together(key_away, value_grad, partner_value)
    got_key = swap(key_away, 2)
    value_away = blocks_for(away_y, value_grad, partner_value)
    value_away, key_grad = together(value_away, key_grad)
    got_value = swap(value_away, 4)
    second = either_term(2)
    got, second = together(got, second)
    total = add(second, *got)
    total, value_grad = together(total, value_grad)
    got = send(2, total, total)
    ahead = terms(*scatter_indices(3))
    ahead, key_grad, value_grad = together(ahead, key_grad, value_grad)
    key_pass = blocks_for(one_y, key_grad, partner_key)
    value_pass = blocks_for(one_x, value_grad, partner_value)
    got, key_pass, value_pass = together(got, key_pass, value_pass)
    up_sum, down_sum = add(ahead[0], got[0]), add(ahead[1], got[1])
    up_sum, down_sum, got_key = together(up_sum, down_sum, got_key)
    up, down = send(3, up_sum, down_sum)
    key_sent = add(key_pass[0], got_key[0])
    key_sent, got_value = together(key_sent, got_value)
    got_key_pass = swap(key_sent, 4)
    value_sent = add(value_pass[0], got_value[0])
    value_sent, key_grad, value_grad = together(value_sent, key_grad, value_grad)
    got_value_pass = swap(value_sent, 2)
    key_own = blocks_for(home, key_grad, partner_key, (got_key,))[0]
    value_own = blocks_for(home, value_grad, partner_value, (got_value,))[0]
    feature_own = terms(here)[0]
    up, key_own, value_own = together(up, key_own, value_own)
    feature_grad = add(feature_own, up, down)
    got_key_pass, feature_grad = together(got_key_pass, feature_grad)
    key_out = (key_own.astype(F32) + got_key_pass.astype(F32)) * norm
    got_value_pass, key_out = together(got_value_pass, key_out)
    value_out = (value_own.astype(F32) + got_value_pass.astype(F32)) * norm
    return attended, query_grad, feature_grad, key_out, value_out


def solution(mesh):
    spread = P("seq", "head")
    return jax.shard_map(
        per_device,
        mesh=mesh,
        in_specs=(spread, P(None, "head"), P(None, "head"), spread, spread, spread),
        out_specs=(spread,) * 5,
        check_vma=False,
    )
```

```python
import functools

import jax
import jax.numpy as jnp
from jax import lax
from jax.experimental import pallas as pl
from jax.experimental.pallas import tpu as pltpu
from jax.sharding import PartitionSpec as P

BF = jnp.bfloat16
F32 = jnp.float32
NT = (((1,), (1,)), ((), ()))
TN = (((0,), (0,)), ((), ()))
MIB = 1024 * 1024


def dot(a, b):
    return jnp.dot(a, b, preferred_element_type=F32)


def dot_nt(a, b):
    return lax.dot_general(a, b, NT, preferred_element_type=F32)


def dot_tn(a, b):
    return lax.dot_general(a, b, TN, preferred_element_type=F32)


def params(limit=16):
    return pltpu.CompilerParams(vmem_limit_bytes=limit * MIB)


def together(*arrays):
    return lax.optimization_barrier(arrays)


SMALL = pl.CostEstimate(flops=1, bytes_accessed=1, transcendentals=0)


def tiles(tokens, causal):
    tile = min(256, tokens)
    for row in range(tokens // tile):
        first, last = row * tile, (row + 1) * tile
        yield slice(first, last), slice(0, last) if causal else slice(first, tokens)


def column(cum_ref, head):
    lanes = lax.broadcasted_iota(jnp.int32, cum_ref.shape, 1)
    return jnp.sum(jnp.where(lanes == head, cum_ref[...], 0.0), axis=1, keepdims=True)


def decay_tile(across, down, rows, seen, causal):
    shape = (rows.stop - rows.start, seen.stop - seen.start)
    one = rows.start + lax.broadcasted_iota(jnp.int32, shape, 0)
    two = seen.start + lax.broadcasted_iota(jnp.int32, shape, 1)
    gap = down[rows] - across[:, seen]
    if causal:
        return jnp.where(two <= one, jnp.exp(gap), 0.0)
    return jnp.where(one <= two, jnp.exp(-gap), 0.0)


def each_head(per, width, body, group=2):
    group = group if per % group == 0 else 1

    def some(number, carry):
        for j in range(group):
            i = number * group + j
            cut = pl.ds(pl.multiple_of(i * width, width), width)
            body(i, pl.program_id(0) * per + i, cut)
        return carry

    lax.fori_loop(0, per // group, some, 0)


def state_kernel(width, per, cum_ref, k_ref, v_ref, s_ref):
    def one(i, head, cut):
        down = column(cum_ref, head)
        tail = jnp.exp(down[-1:] - down)
        scaled = (k_ref[:, cut].astype(F32) * tail).astype(BF)
        s_ref[i] = dot_tn(scaled, v_ref[:, cut]).astype(BF)

    each_head(per, width, one, 4)


def local_kernel(width, per, cum_ref, cumt_ref, q_ref, k_ref, v_ref, mix_ref):
    def one(i, head, cut):
        down, across = column(cum_ref, head), cumt_ref[pl.ds(head, 1), :]
        for rows, seen in tiles(q_ref.shape[0], True):
            scores = dot_nt(q_ref[rows, cut], k_ref[seen, cut])
            weights = (scores * decay_tile(across, down, rows, seen, True)).astype(BF)
            mix_ref[rows, cut] = dot(weights, v_ref[seen, cut]).astype(mix_ref.dtype)

    each_head(per, width, one, 4)


def norm_kernel(width, per, cum_ref, q_ref, g_ref, mix_ref, s_ref, att_ref, hg_ref, r_ref):
    def one(i, head, cut):
        grow = jnp.exp(column(cum_ref, head))
        carried = grow * dot(q_ref[:, cut], s_ref[i])
        mixed = mix_ref[:, cut].astype(F32) + carried
        grad = g_ref[:, cut].astype(F32)
        scale = lax.rsqrt(jnp.mean(mixed * mixed, axis=-1, keepdims=True) + 1e-06)
        projection = jnp.mean(grad * mixed, axis=-1, keepdims=True)
        att_ref[:, cut] = (mixed * scale).astype(BF)
        head_grad = (scale * grad - mixed * (scale * scale * scale * projection)).astype(BF)
        hg_ref[:, cut] = head_grad
        grown = (q_ref[:, cut].astype(F32) * grow).astype(BF)
        r_ref[i] = dot_tn(grown, head_grad).astype(BF)

    each_head(per, width, one, 4)


def back_query_kernel(width, per, cum_ref, cumt_ref, k_ref, v_ref, hg_ref, s_ref, qg_ref):
    def one(i, head, cut):
        down, across = column(cum_ref, head), cumt_ref[pl.ds(head, 1), :]
        grow = jnp.exp(down)
        for rows, seen in tiles(k_ref.shape[0], True):
            pairs = dot_nt(hg_ref[rows, cut], v_ref[seen, cut])
            pairs = (pairs * decay_tile(across, down, rows, seen, True)).astype(BF)
            carried = grow[rows] * dot_nt(hg_ref[rows, cut], s_ref[i])
            qg_ref[rows, cut] = (dot(pairs, k_ref[seen, cut]) + carried).astype(BF)

    each_head(per, width, one, 4)


def back_keys_kernel(width, per, cum_ref, cumt_ref, q_ref, k_ref, v_ref, hg_ref, kg_ref, vg_ref):
    def one(i, head, cut):
        down, across = column(cum_ref, head), cumt_ref[pl.ds(head, 1), :]
        for rows, seen in tiles(q_ref.shape[0], False):
            decay = decay_tile(across, down, rows, seen, False)
            pairs = (dot_nt(v_ref[rows, cut], hg_ref[seen, cut]) * decay).astype(BF)
            kg_ref[rows, cut] = dot(pairs, q_ref[seen, cut]).astype(kg_ref.dtype)
            weights = (dot_nt(k_ref[rows, cut], q_ref[seen, cut]) * decay).astype(BF)
            vg_ref[rows, cut] = dot(weights, hg_ref[seen, cut]).astype(vg_ref.dtype)

    each_head(per, width, one)


def close_kernel(width, per, cum_ref, k_ref, v_ref, kl_ref, vl_ref, r_ref, kg_ref, vg_ref):
    def one(i, head, cut):
        down = column(cum_ref, head)
        tail = jnp.exp(down[-1:] - down)
        key_carried = tail * dot_nt(v_ref[:, cut], r_ref[i])
        value_carried = tail * dot(k_ref[:, cut], r_ref[i])
        kg_ref[:, cut] = (kl_ref[:, cut].astype(F32) + key_carried).astype(BF)
        vg_ref[:, cut] = (vl_ref[:, cut].astype(F32) + value_carried).astype(BF)

    each_head(per, width, one, 4)


def per_head(kernel, args, kinds, outs, tokens, heads, width, per, name, limit=60):
    specs = {
        "cum": pl.BlockSpec((tokens, heads), lambda j: (0, 0)),
        "cumt": pl.BlockSpec((heads, tokens), lambda j: (0, 0)),
        "col": pl.BlockSpec((tokens, width * per), lambda j: (0, j)),
        "state": pl.BlockSpec((per, width, width), lambda j: (j, 0, 0)),
    }
    shapes = {"col": (tokens, heads * width), "state": (heads, width, width)}
    return pl.pallas_call(
        functools.partial(kernel, width, per),
        grid=(heads // per,),
        in_specs=[specs[k] for k in kinds],
        out_specs=[specs[k] for k in outs],
        out_shape=[jax.ShapeDtypeStruct(shapes[k], BF) for k in outs],
        compiler_params=params(limit),
        cost_estimate=SMALL,
        name=name,
    )(*args)


def feature_kernel(index_ref, kg_ref, vg_ref, kw_ref, vw_ref, out_ref):
    grads = jnp.concatenate([kg_ref[...], vg_ref[...]], axis=1)
    weights = jnp.concatenate([kw_ref[...], vw_ref[...]], axis=1)
    out_ref[0] = dot_nt(grads, weights).astype(BF)


def feature_terms(indices, key_grad, value_grad, key_weight, value_weight, span):
    tokens, proj = key_grad.shape
    tile = min(512, span)
    steps = span // tile
    number = indices.shape[0]
    whole = pl.BlockSpec((tokens, proj), lambda i, j, d: (0, 0))
    weight = pl.BlockSpec((tile, proj), lambda i, j, d: (d[i] * steps + j, 0))
    return pl.pallas_call(
        feature_kernel,
        grid_spec=pltpu.PrefetchScalarGridSpec(
            num_scalar_prefetch=1,
            grid=(number, steps),
            in_specs=[whole, whole, weight, weight],
            out_specs=pl.BlockSpec((1, tokens, tile), lambda i, j, d: (i, 0, j)),
        ),
        out_shape=jax.ShapeDtypeStruct((number, tokens, span), BF),
        compiler_params=params(60),
        cost_estimate=SMALL,
        name="feature_terms",
    )(indices, key_grad, value_grad, key_weight, value_weight)


def weight_kernel(count, index_ref, fo_ref, fp_ref, go_ref, gp_ref, *refs):
    turned = jnp.concatenate([fo_ref[0], fp_ref[0]], axis=1)
    total = dot(turned, jnp.concatenate([go_ref[...], gp_ref[...]], axis=0))
    for r in refs[:count]:
        total += r[0].astype(F32)
    refs[count][0] = total.astype(BF)


def weight_terms(slots, own_t, partner_t, grad, partner_grad, adds=()):
    tokens, proj = grad.shape
    span = own_t.shape[1]
    number = slots.shape[0]
    tile = proj
    rows = pl.BlockSpec((1, span, tokens), lambda j, i, d: (d[i], 0, 0))
    cols = pl.BlockSpec((tokens, tile), lambda j, i, d: (0, j))
    extra = [
        pl.BlockSpec((1, span, tile), lambda j, i, d, last=a.shape[0] - 1: (last, 0, j)) for a in adds
    ]
    return pl.pallas_call(
        functools.partial(weight_kernel, len(adds)),
        grid_spec=pltpu.PrefetchScalarGridSpec(
            num_scalar_prefetch=1,
            grid=(proj // tile, number),
            in_specs=[rows, rows, cols, cols] + extra,
            out_specs=pl.BlockSpec((1, span, tile), lambda j, i, d: (i, 0, j)),
        ),
        out_shape=jax.ShapeDtypeStruct((number, span, proj), BF),
        compiler_params=params(60),
        cost_estimate=SMALL,
        name="weight_terms",
    )(slots, own_t, partner_t, grad, partner_grad, *adds)


def turn_kernel(aliased, core_ref, *refs):
    shards, (own_ref, other_ref, held, turned, sem) = refs[aliased:-5], refs[-5:]
    core = core_ref[0]
    for i, shard in enumerate(shards):

        @pl.when(pl.program_id(0) == i)
        def _():
            copy = pltpu.make_async_copy(shard, held, sem)
            copy.start()
            copy.wait()

    turned[...] = held[...].T
    rows = own_ref.shape[1]
    own_ref[0] = turned[pl.ds(pl.multiple_of(core * rows, rows), rows), :]
    other_ref[0] = turned[pl.ds(pl.multiple_of((1 - core) * rows, rows), rows), :]


def turn_features(core, shards, first, slots, held=()):
    tokens, depth = shards[0].shape
    half = pl.BlockSpec((1, depth // 2, tokens), lambda j, d: (first + j, 0, 0))
    aliased = len(held)
    return pl.pallas_call(
        functools.partial(turn_kernel, aliased),
        grid_spec=pltpu.PrefetchScalarGridSpec(
            num_scalar_prefetch=1,
            grid=(len(shards),),
            in_specs=[pl.BlockSpec(memory_space=pl.ANY)] * (aliased + len(shards)),
            out_specs=[half, half],
            scratch_shapes=[
                pltpu.VMEM((tokens, depth), BF),
                pltpu.VMEM((depth, tokens), BF),
                pltpu.SemaphoreType.DMA,
            ],
        ),
        out_shape=[jax.ShapeDtypeStruct((slots, depth // 2, tokens), BF)] * 2,
        input_output_aliases={1 + i: i for i in range(aliased)},
        compiler_params=params(60),
        cost_estimate=SMALL,
        name="turn_features",
    )(core[None], *held, *shards)


def merge_states(earlier, later):
    return (earlier[0] * later[0], later[0][:, None, None] * earlier[1] + later[1])


def entering(x, axis, backward):
    count = lax.axis_size(axis)
    place = lax.axis_index(axis)
    ahead = count - 1 - place if backward else place
    gathered = tuple(lax.all_gather(a.astype(BF), axis) for a in x)
    state = (jnp.ones_like(x[0]), jnp.zeros_like(x[1]))

    def one(hop, state):
        source = count - 1 - hop if backward else hop
        item = tuple(
            lax.dynamic_index_in_dim(a, source, 0, False).astype(own.dtype)
            for a, own in zip(gathered, x)
        )
        return merge_states(state, item)

    return lax.fori_loop(0, ahead, one, state)[1].astype(BF)


def swap(x, bit, keep=None):
    pairs = [(s, s ^ bit) for s in range(8) if keep is None or keep(s)]
    return lax.ppermute(x, "seq", pairs)


def gather_totals(own):
    place = lax.axis_index("seq")
    held = own[None]
    for bit in (1, 2, 4):
        other = swap(held, bit)
        upper = (place & bit) != 0
        held = jnp.concatenate(
            [jnp.where(upper, other, held), jnp.where(upper, held, other)], axis=0
        )
    return held


def entering_chips(state, totals, backward, first_wait, second_wait):
    place = lax.axis_index("seq")
    core = lax.rem(place, 2)
    half = state.shape[0] // 2
    ahead_of = (lambda bit: (place & bit) == 0) if backward else (lambda bit: (place & bit) != 0)
    decay = jnp.exp(totals)[:, :, None, None]

    def halves(a):
        return lax.dynamic_slice_in_dim(a, core * half, half, 0)

    def join(own, other, bit, own_factor, other_factor):
        late = ahead_of(bit)
        own, other = own.astype(F32), other.astype(F32)
        return jnp.where(late, own_factor * other + own, other_factor * own + other)

    partner = swap(state, 1)
    own_decay, partner_decay = decay[place], decay[place ^ 1]
    chip = join(halves(state), halves(partner), 1, halves(own_decay), halves(partner_decay)).astype(BF)
    beside, first_wait = together(swap(chip, 2), first_wait)
    chip_decay = halves(own_decay * partner_decay)
    beside_decay = halves(decay[place ^ 2] * decay[place ^ 3])
    pair = join(chip, beside, 2, chip_decay, beside_decay).astype(BF)
    keep = (lambda s: (s & 4) != 0) if backward else (lambda s: (s & 4) == 0)
    passed, second_wait = together(swap(pair, 4, keep), second_wait)
    passed = passed.astype(F32)
    entered = jnp.where(ahead_of(2), beside_decay * passed + beside.astype(F32), passed).astype(BF)
    other = swap(entered, 1)
    whole = jnp.where(
        core == 0, jnp.concatenate([entered, other]), jnp.concatenate([other, entered])
    )
    step = partner_decay * whole.astype(F32) + partner.astype(F32)
    return jnp.where(ahead_of(1), step.astype(BF), whole), first_wait, second_wait


def line_pairs(count, step, up):
    if up:
        return [(i, i + 1) for i in range(step - 1, count - 1)]
    return [(i, i - 1) for i in range(1, count - step + 1)]


def scatter_pairs(count, step, up):
    if up:
        return [(i, i + 1) for i in range(0, min(step, count - 1))]
    return [(i, i - 1) for i in range(max(1, count - step), count)]


def per_device(features, key_weight, value_weight, queries, log_decay, out_grad):
    tokens, proj = queries.shape
    depth = features.shape[1]
    model = key_weight.shape[0]
    heads = log_decay.shape[1]
    width = proj // heads
    per = 4 if heads % 4 == 0 else 1
    count = lax.axis_size("head")
    blocks = lax.axis_size("seq")
    here = lax.axis_index("head")
    place = lax.axis_index("seq")
    chips = blocks == 8 and model == 8 * 512 and count == 4

    cum = jnp.cumsum(log_decay, axis=0)
    cum_t = cum.T
    total = cum[-1]

    up = down = features

    def rows_of(weight, index):
        return lax.dynamic_slice_in_dim(weight, index * depth, depth, 0)

    def project(sums, shard, key_rows, value_rows):
        parts = [dot(shard, key_rows), dot(shard, value_rows)]
        return parts if sums is None else [a + b for a, b in zip(sums, parts)]

    def both_rows(index):
        return rows_of(key_weight, index), rows_of(value_weight, index)

    if chips:
        core = lax.rem(place, 2)
        totals = gather_totals(total)
        chip = place // 2

        def slots_of(*targets):
            offsets = jnp.stack(targets) - here
            far = jnp.abs(offsets)
            return jnp.where(far < 2, jnp.where(offsets < 0, 2, far), far + 1)

        ranks = (
            slots_of(chip ^ 3, chip ^ 1),
            slots_of(chip ^ 3, chip ^ 2),
            slots_of(chip ^ 1),
            slots_of(chip ^ 2),
            slots_of(chip),
        )
    sums = project(None, features, *both_rows(here))
    slots = [features]
    turned = ()
    merged = None
    for step in range(1, count):
        upward, downward = line_pairs(count, step, True), line_pairs(count, step, False)
        if merged is None:
            up = lax.ppermute(up, "head", upward)
            down = lax.ppermute(down, "head", downward)
            got = [up, down]
        else:
            got = [lax.ppermute(merged, "head", upward + downward)]
        if 2 * step >= count:
            index = jnp.where(here >= step, here - step, jnp.minimum(here + step, count - 1))
            rows = [both_rows(index)]
        else:
            rows = [
                both_rows(jnp.minimum(here + step, count - 1)),
                both_rows(jnp.maximum(here - step, 0)),
            ]
        if chips and step == count - 2:
            turned = turn_features(core, slots, 0, 5)
            got, sums, turned, totals, ranks, cum, cum_t = together(
                got, sums, turned, totals, ranks, cum, cum_t
            )
        elif step == count - 1:
            got, sums, rows = together(got, sums, rows)
        else:
            got, sums = together(got, sums)
        if 2 * step >= count:
            merged = got[0] if len(got) == 1 else got[0] + got[1]
            shards = [merged]
        else:
            up, down = got
            shards = [down, up]
        slots += shards
        for shard, pair in zip(shards, rows):
            sums = project(sums, shard, *pair)
    key_sum, value_sum = sums
    keys, values = key_sum.astype(BF), value_sum.astype(BF)

    each = functools.partial(per_head, tokens=tokens, heads=heads, width=width, per=per)
    (local_state,) = each(
        state_kernel,
        (cum, keys, values),
        ("cum", "col", "col"),
        ("state",),
        name="local_state",
        limit=16,
    )
    (mix,) = each(
        local_kernel,
        (cum, cum_t, queries, keys, values),
        ("cum", "cumt", "col", "col", "col"),
        ("col",),
        name="local_mix",
    )
    if chips:
        own_t, other_t = turn_features(core, slots[3:], 3, 5, turned)
        incoming, mix, (own_t, other_t) = entering_chips(
            local_state, totals, False, mix, (own_t, other_t)
        )
        incoming, other_t = together(incoming, other_t)
        partner_t = swap(other_t, 1)
    else:
        incoming = entering((jnp.exp(total), local_state.astype(F32)), "seq", False)
    attended, head_grad, local_reverse = each(
        norm_kernel,
        (cum, queries, out_grad, mix, incoming),
        ("cum", "col", "col", "col", "state"),
        ("col", "col", "state"),
        name="norm_grad",
    )
    (query_grad,) = each(
        back_query_kernel,
        (cum, cum_t, keys, values, head_grad, incoming),
        ("cum", "cumt", "col", "col", "col", "state"),
        ("col",),
        name="back_query",
    )
    key_local, value_local = each(
        back_keys_kernel,
        (cum, cum_t, queries, keys, values, head_grad),
        ("cum", "cumt", "col", "col", "col", "col"),
        ("col", "col"),
        name="back_keys",
    )
    if chips:
        outgoing, query_grad, (key_local, value_local, partner_t) = entering_chips(
            local_reverse, totals, True, query_grad, (key_local, value_local, partner_t)
        )
    else:
        outgoing = entering((jnp.exp(total), local_reverse.astype(F32)), "seq", True)
    key_grad, value_grad = each(
        close_kernel,
        (cum, keys, values, key_local, value_local, outgoing),
        ("cum", "col", "col", "col", "col", "state"),
        ("col", "col"),
        name="close_back",
    )

    def terms(*indices):
        return feature_terms(
            jnp.stack(indices), key_grad, value_grad, key_weight, value_weight, depth
        )

    def add(*terms):
        return sum(t.astype(F32) for t in terms).astype(BF)

    def scatter_indices(step):
        upward = jnp.minimum(here + count - step, count - 1)
        downward = jnp.maximum(here - count + step, 0)
        return upward, downward

    def either_term(step):
        upward, downward = scatter_indices(step)
        return terms(jnp.where(here < step, upward, downward))[0]

    def send(step, up_sum, down_sum):
        upward, downward = scatter_pairs(count, step, True), scatter_pairs(count, step, False)
        if 2 * step < count - 1:
            return (lax.ppermute(up_sum, "head", upward + downward),)
        return lax.ppermute(up_sum, "head", upward), lax.ppermute(down_sum, "head", downward)

    norm = (tokens * blocks) ** (-0.5)
    if not chips:
        got = ()
        for step in range(1, count):
            if 2 * step <= count:
                total = add(either_term(step), *got)
                got = send(step, total, total)
            else:
                up_term, down_term = terms(*scatter_indices(step))
                got = send(step, add(up_term, got[0]), add(down_term, got[1]))
        feature_grad = add(terms(here)[0], *got)
        gathered = lax.all_gather(features, "head", axis=1, tiled=True)
        both = jnp.concatenate([key_grad, value_grad], axis=1)
        summed = lax.psum_scatter(
            lax.dot_general(gathered, both, TN, preferred_element_type=F32).astype(BF),
            "seq",
            scatter_dimension=0,
            tiled=True,
        ).astype(F32)
        summed = summed * norm
        return attended, query_grad, feature_grad, summed[:, :proj], summed[:, proj:]

    away_x, away_y, one_x, one_y, home = ranks
    partner_key, partner_value = swap(key_grad, 1), swap(value_grad, 1)

    def blocks_for(slot, grad, partner_grad, adds=()):
        return weight_terms(slot, own_t, partner_t, grad, partner_grad, adds)

    first = either_term(1)
    got = send(1, first, first)
    key_away = blocks_for(away_x, key_grad, partner_key)
    key_away, value_grad, partner_value = together(key_away, value_grad, partner_value)
    got_key = swap(key_away, 2)
    value_away = blocks_for(away_y, value_grad, partner_value)
    value_away, key_grad = together(value_away, key_grad)
    got_value = swap(value_away, 4)
    second = either_term(2)
    got, second = together(got, second)
    total = add(second, *got)
    total, value_grad = together(total, value_grad)
    got = send(2, total, total)
    ahead = terms(*scatter_indices(3))
    ahead, key_grad, value_grad = together(ahead, key_grad, value_grad)
    key_pass = blocks_for(one_y, key_grad, partner_key)
    value_pass = blocks_for(one_x, value_grad, partner_value)
    got, key_pass, value_pass = together(got, key_pass, value_pass)
    up_sum, down_sum = add(ahead[0], got[0]), add(ahead[1], got[1])
    up_sum, down_sum, got_key = together(up_sum, down_sum, got_key)
    up, down = send(3, up_sum, down_sum)
    key_sent = add(key_pass[0], got_key[0])
    key_sent, got_value = together(key_sent, got_value)
    got_key_pass = swap(key_sent, 4)
    value_sent = add(value_pass[0], got_value[0])
    value_sent, key_grad, value_grad = together(value_sent, key_grad, value_grad)
    got_value_pass = swap(value_sent, 2)
    key_own = blocks_for(home, key_grad, partner_key, (got_key,))[0]
    value_own = blocks_for(home, value_grad, partner_value, (got_value,))[0]
    feature_own = terms(here)[0]
    up, key_own, value_own = together(up, key_own, value_own)
    feature_grad = add(feature_own, up, down)
    got_key_pass, feature_grad = together(got_key_pass, feature_grad)
    key_out = (key_own.astype(F32) + got_key_pass.astype(F32)) * norm
    got_value_pass, key_out = together(got_value_pass, key_out)
    value_out = (value_own.astype(F32) + got_value_pass.astype(F32)) * norm
    return attended, query_grad, feature_grad, key_out, value_out


def solution(mesh):
    spread = P("seq", "head")
    return jax.shard_map(
        per_device,
        mesh=mesh,
        in_specs=(spread, P(None, "head"), P(None, "head"), spread, spread, spread),
        out_specs=(spread,) * 5,
        check_vma=False,
    )
```
